512 devices in a mesh: strike: 64 (over z, x, core), depth: 8 (over y).
Axes of the slice: x: 4, y: 8, z: 8, core: 2. Of those that a mesh axis runs over, the one named last changes fastest.
Arguments:
- state_dofs: float32 [9, 56, 16384], P(None, None, ('strike', 'depth')), may hold values from -6 to 6
- jacobians: float32 [3, 9, 9, 16384], P(None, None, None, ('strike', 'depth')), may hold values from -2.1 to 2.1
- flux_local: float32 [4, 9, 9, 16384], P(None, None, None, ('strike', 'depth')), may hold values from -1 to 1
- flux_neigh: float32 [4, 9, 9, 16384], P(None, None, None, ('strike', 'depth')), may hold values from -1 to 1
- stiffness: float32 [3, 56, 56], replicated, may hold values from -0.75 to 0.75
- volume: float32 [3, 56, 56], replicated, may hold values from -0.75 to 0.75
- face_proj: float32 [12, 56, 21], replicated, may hold values from -0.75 to 0.75
- face_lift: float32 [4, 21, 56], replicated, may hold values from -1.25 to 1.25
- strength: float32 [16384], P(('strike', 'depth')), may hold values from 0.3 to 3
- cluster: int32 [16384], P(('strike', 'depth')), may hold values from 0 to 1, as said below
- neighbours: int32 [4, 16384], P(None, ('strike', 'depth')), may hold values from 0 to 128, as said below
- face_orient: int32 [4, 16384], P(None, ('strike', 'depth')), may hold values from 0 to 11
- strike_sends: int32 [2, 16384], P(None, ('strike', 'depth')), may hold values from 0 to 31
- strike_orient: int32 [2, 16384], P(None, ('strike', 'depth')), may hold values from 0 to 11
- depth_sends: int32 [2, 8192], P(None, ('strike', 'depth')), may hold values from 0 to 31
- depth_orient: int32 [2, 8192], P(None, ('strike', 'depth')), may hold values from 0 to 11
- fault_elem: int32 [16384], P(('strike', 'depth')), may hold values from 0 to 31
- fault_proj: int32 [16384], P(('strike', 'depth')), may hold values from 0 to 11
Outputs:
- new_dofs: float32 [9, 56, 16384], P(None, None, ('strike', 'depth'))
The draws below stay inside these ranges and needn't reach their ends.
Inputs may be any that keep to these rules, and one draw needn't show every extreme that they name: 0 marks the fast cluster, 1 the slow one; at most 16 elements of one device are in the fast cluster, and some device has exactly 16. `neighbours`: every received face of a device is named by exactly one face of that device; the largest value marks the slab's outer boundary and occurs on every device.
All inputs are finite; a program needn't handle non-finite values.
Results may differ from the reference program's by a relative error of at most 0.0003.
Values sent between devices are 32-bit elements; how exact they have to be, the bound alone decides.
No kernel may reach another device: no remote copies, remote signals or barrier semaphores. Data moves between devices by JAX's collectives and lax.ppermute only.
A program may use at most 64 MiB of HBM per device.

```python
import math
import jax
import jax.numpy as jnp
from jax import lax

QUANT = 9
BASIS = 56
FACE_BASIS = 21
ORDER = 6
PROJS = 12
ELEM_DEV = 32
FAULT_DEV = 32
FAST_DEV = 16
STRIKE_SLOTS = 32
DEPTH_SLOTS = 16
ELEMS = 16384
STRIKE_TOTAL = 16384
DEPTH_TOTAL = 8192
FAULTS = 16384
N_STRIKE = 64
N_DEPTH = 8


def shuffled(device_key):
    return jax.random.permutation(device_key, ELEM_DEV)


def draw_cluster(key, part):
    key = jax.random.fold_in(key, 5)
    devices = ELEMS // ELEM_DEV
    count_key, full_key, order_key = jax.random.split(key, 3)
    counts = jax.random.randint(count_key, (devices,), FAST_DEV // 8, FAST_DEV // 2 + 1)
    busiest = jax.random.randint(full_key, (), 0, devices)
    counts = jnp.where(jnp.arange(devices) == busiest, FAST_DEV, counts)
    positions = jax.vmap(shuffled)(jax.random.split(order_key, devices))
    return jnp.where(positions < counts[:, None], 0, 1).astype(jnp.int32).reshape(ELEMS)


def neighbour_block(device_key):
    halo_count = 2 * STRIKE_SLOTS + 2 * DEPTH_SLOTS
    edge_count = ELEM_DEV // 8
    order_key, local_key = jax.random.split(device_key)
    places = jax.random.permutation(order_key, 4 * ELEM_DEV)
    local_ids = jax.random.randint(local_key, (4 * ELEM_DEV,), 0, ELEM_DEV)
    slot_ids = jnp.where(places < halo_count, ELEM_DEV + places, jnp.where(places < halo_count + edge_count, ELEM_DEV + halo_count, local_ids))
    return slot_ids.reshape(4, ELEM_DEV)


def draw_neighbours(key, part):
    key = jax.random.fold_in(key, 23)
    devices = ELEMS // ELEM_DEV
    blocks = jax.vmap(neighbour_block)(jax.random.split(key, devices))
    return jnp.transpose(blocks, (1, 0, 2)).reshape(4, ELEMS).astype(jnp.int32)


def touch_ends(entries, own_key, low, largest):
    longest = entries.shape.index(max(entries.shape))
    spots = []
    for shift in (0, 1):
        where = [jax.random.randint(jax.random.fold_in(own_key, axis), (), 0, length) for axis, length in enumerate(entries.shape)]
        where[longest] = (where[longest] + shift) % entries.shape[longest]
        spots.append(tuple(where))
    return entries.at[spots[0]].set(low).at[spots[1]].set(largest)


def levels(stream_key, dims, pieces, smallest, high):
    level = 1.0
    for position, parts in pieces:
        draws = jax.random.uniform(jax.random.fold_in(jax.random.fold_in(stream_key, 6), position), (parts,), jnp.float32, smallest / len(pieces), high / len(pieces))
        level = level * jnp.repeat(jnp.exp(draws), dims[position] // parts).reshape((-1,) + (1,) * (len(dims) - 1 - position))
    return level


def centred(key, dims, width, most, shards=(), held_as=jnp.bfloat16):
    array = width * jax.random.normal(key, dims, jnp.float32)
    if shards:
        array = array * levels(key, dims, shards, -0.22, 0.18)
    return jnp.clip(array, -most, most).astype(held_as)


def setup_inputs(seed: int = 0) -> dict:
    streams_of = jax.random.split(jax.random.key(seed), 19)
    state_dofs = centred(streams_of[0], (QUANT, BASIS, ELEMS), 1.0, 6.0, ((2, 512),), jnp.float32)
    jacobians = centred(streams_of[1], (3, QUANT, QUANT, ELEMS), 0.35, 2.1, ((3, 512),), jnp.float32)
    flux_local = centred(streams_of[2], (4, QUANT, QUANT, ELEMS), (4 * QUANT) ** -0.5, 1.0, ((3, 512),), jnp.float32)
    flux_neigh = centred(streams_of[3], (4, QUANT, QUANT, ELEMS), (4 * QUANT) ** -0.5, 1.0, ((3, 512),), jnp.float32)
    stiffness = centred(streams_of[4], (3, BASIS, BASIS), BASIS ** -0.5, 0.75, (), jnp.float32)
    volume = centred(streams_of[5], (3, BASIS, BASIS), BASIS ** -0.5, 0.75, (), jnp.float32)
    face_proj = centred(streams_of[6], (PROJS, BASIS, FACE_BASIS), BASIS ** -0.5, 0.75, (), jnp.float32)
    face_lift = centred(streams_of[7], (4, FACE_BASIS, BASIS), FACE_BASIS ** -0.5, 1.25, (), jnp.float32)
    strength = jnp.clip(jnp.exp(math.log(3.0) - 2.3025851 * jax.random.uniform(streams_of[8], (FAULTS,), jnp.float32) ** levels(streams_of[8], (FAULTS,), ((0, 512),), -0.2, 0.2)), 0.3, 3.0)
    cluster = draw_cluster(jax.random.fold_in(streams_of[18], 71), 0)
    neighbours = draw_neighbours(jax.random.fold_in(streams_of[18], 71), 0)
    face_orient = touch_ends(jax.random.randint(streams_of[11], (4, ELEMS), 0, PROJS), jax.random.fold_in(streams_of[11], 1), 0, PROJS - 1).astype(jnp.int32)
    strike_sends = touch_ends(jax.random.randint(streams_of[12], (2, STRIKE_TOTAL), 0, ELEM_DEV), jax.random.fold_in(streams_of[12], 1), 0, ELEM_DEV - 1).astype(jnp.int32)
    strike_orient = touch_ends(jax.random.randint(streams_of[13], (2, STRIKE_TOTAL), 0, PROJS), jax.random.fold_in(streams_of[13], 1), 0, PROJS - 1).astype(jnp.int32)
    depth_sends = touch_ends(jax.random.randint(streams_of[14], (2, DEPTH_TOTAL), 0, ELEM_DEV), jax.random.fold_in(streams_of[14], 1), 0, ELEM_DEV - 1).astype(jnp.int32)
    depth_orient = touch_ends(jax.random.randint(streams_of[15], (2, DEPTH_TOTAL), 0, PROJS), jax.random.fold_in(streams_of[15], 1), 0, PROJS - 1).astype(jnp.int32)
    fault_elem = touch_ends(jax.random.randint(streams_of[16], (FAULTS,), 0, ELEM_DEV), jax.random.fold_in(streams_of[16], 1), 0, ELEM_DEV - 1).astype(jnp.int32)
    fault_proj = touch_ends(jax.random.randint(streams_of[17], (FAULTS,), 0, PROJS), jax.random.fold_in(streams_of[17], 1), 0, PROJS - 1).astype(jnp.int32)
    return {"state_dofs": state_dofs, "jacobians": jacobians, "flux_local": flux_local, "flux_neigh": flux_neigh, "stiffness": stiffness, "volume": volume, "face_proj": face_proj, "face_lift": face_lift, "strength": strength, "cluster": cluster, "neighbours": neighbours, "face_orient": face_orient, "strike_sends": strike_sends, "strike_orient": strike_orient, "depth_sends": depth_sends, "depth_orient": depth_orient, "fault_elem": fault_elem, "fault_proj": fault_proj}


highest = lax.Precision.HIGHEST
fast_step = 0.5

def derivative_step(current, jacobians, stiffness):
    applied = jnp.einsum('qce,dcb->dqbe', current, stiffness, precision=highest)
    return -jnp.einsum('dpqe,dqbe->pbe', jacobians, applied, precision=highest)

def integrals(state_block, jacobians, stiffness, with_second):
    first_half = jnp.zeros_like(state_block)
    second_half = jnp.zeros_like(state_block)
    current = state_block
    factorial = 1.0
    for degree in range(ORDER):
        factorial = factorial * (degree + 1)
        early_power = fast_step ** (degree + 1)
        late_power = (2.0 * fast_step) ** (degree + 1) - early_power
        first_half = first_half + current * (early_power / factorial)
        if with_second:
            second_half = second_half + current * (late_power / factorial)
        if degree + 1 < ORDER:
            current = derivative_step(current, jacobians, stiffness)
    return (first_half, second_half)

def project_all(values, face_proj):
    return jnp.einsum('pbe,mbk->pkme', values, face_proj, precision=highest)

def face_traces(proj_table, halo, neighbours, face_orient):
    elem_count = proj_table.shape[3]
    flat_table = proj_table.reshape(QUANT, FACE_BASIS, PROJS * elem_count)
    all_columns = jnp.concatenate([flat_table, halo, jnp.zeros((QUANT, FACE_BASIS, 1), jnp.float32)], axis=2)
    column_index = jnp.where(neighbours < elem_count, face_orient * elem_count + neighbours, PROJS * elem_count + neighbours - elem_count)
    return jnp.take(all_columns, column_index, axis=2)

def update(values, proj_table, traces, jacobians, flux_local, flux_neigh, volume, face_lift):
    applied = jnp.einsum('pbe,dbc->dpce', values, volume, precision=highest)
    interior = jnp.einsum('dqpe,dpce->qce', jacobians, applied, precision=highest)
    own_faces = jnp.einsum('fqpe,pkfe->fqke', flux_local, proj_table[:, :, 0::3, :], precision=highest)
    local_flux = jnp.einsum('fqke,fkb->qbe', own_faces, face_lift, precision=highest)
    other_faces = jnp.einsum('fqpe,pkfe->fqke', flux_neigh, traces, precision=highest)
    neighbour_flux = jnp.einsum('fqke,fkb->qbe', other_faces, face_lift, precision=highest)
    return interior - local_flux - neighbour_flux

def fault_correction(own_trace, other_trace, fault_side, strength, face_lift, fault_proj, fault_elem, elem_count):
    shear_one = 0.5 * (own_trace[3] + other_trace[3]) + fault_side * 0.5 * (other_trace[7] - own_trace[7])
    shear_two = 0.5 * (own_trace[5] + other_trace[5]) + fault_side * 0.5 * (other_trace[8] - own_trace[8])
    magnitude = jnp.sqrt(shear_one * shear_one + shear_two * shear_two)
    factor = strength[None, :] / jnp.maximum(magnitude, strength[None, :])
    traction_one = shear_one * factor
    traction_two = shear_two * factor
    empty_rows = jnp.zeros_like(shear_one)
    jump_rows = jnp.stack([empty_rows, empty_rows, empty_rows, traction_one, empty_rows, traction_two, empty_rows, fault_side * (traction_one - shear_one), fault_side * (traction_two - shear_two)])
    lifted = jnp.einsum('pks,fkb->fpbs', jump_rows, face_lift, precision=highest)
    face_pick = (fault_proj[None, :] // 3 == jnp.arange(4, dtype=jnp.int32)[:, None]).astype(jnp.float32)
    chosen = lax.optimization_barrier(jnp.sum(lifted * face_pick[:, None, None, :], axis=0))
    placing = (fault_elem[:, None] == jnp.arange(elem_count, dtype=jnp.int32)[None, :]).astype(jnp.float32)
    return jnp.einsum('pbs,se->pbe', chosen, placing, precision=highest)

def device_block(source, device, block_width):
    return lax.dynamic_slice_in_dim(source, device * block_width, block_width, source.ndim - 1)

def outgoing(proj_table, sends, orients):
    elem_count = proj_table.shape[3]
    flat_table = proj_table.reshape(QUANT, FACE_BASIS, PROJS * elem_count)
    return jnp.take(flat_table, orients * elem_count + sends, axis=2)

def arrivals(strike_all, depth_all, device):
    devices = N_STRIKE * N_DEPTH
    strike_pos = device // N_DEPTH
    depth_pos = device % N_DEPTH
    lower_strike = jnp.where(strike_pos > 0, strike_all[jnp.maximum(device - N_DEPTH, 0)][:, :, 1], 0.0)
    upper_strike = jnp.where(strike_pos < N_STRIKE - 1, strike_all[jnp.minimum(device + N_DEPTH, devices - 1)][:, :, 0], 0.0)
    lower_depth = jnp.where(depth_pos > 0, depth_all[jnp.maximum(device - 1, 0)][:, :, 1], 0.0)
    upper_depth = jnp.where(depth_pos < N_DEPTH - 1, depth_all[jnp.minimum(device + 1, devices - 1)][:, :, 0], 0.0)
    return jnp.concatenate([lower_strike, upper_strike, lower_depth, upper_depth], axis=2)

def reference(state_dofs, jacobians, flux_local, flux_neigh, stiffness, volume, face_proj, face_lift, strength, cluster, neighbours, face_orient, strike_sends, strike_orient, depth_sends, depth_orient, fault_elem, fault_proj):
    devices = N_STRIKE * N_DEPTH
    device_ids = jnp.arange(devices, dtype=jnp.int32)

    def sends_of(proj_table, device):
        strike_out = outgoing(proj_table, device_block(strike_sends, device, STRIKE_SLOTS), device_block(strike_orient, device, STRIKE_SLOTS))
        depth_out = outgoing(proj_table, device_block(depth_sends, device, DEPTH_SLOTS), device_block(depth_orient, device, DEPTH_SLOTS))
        return (strike_out, depth_out)

    def phase_one(device):
        state_block = device_block(state_dofs, device, ELEM_DEV)
        jac_block = device_block(jacobians, device, ELEM_DEV)
        first_half, second_half = integrals(state_block, jac_block, stiffness, True)
        strike_out, depth_out = sends_of(project_all(first_half, face_proj), device)
        return (first_half, second_half, strike_out, depth_out)
    firsts, seconds, strike_first, depth_first = lax.map(phase_one, device_ids)

    def phase_two(device):
        state_block = device_block(state_dofs, device, ELEM_DEV)
        jac_block = device_block(jacobians, device, ELEM_DEV)
        first_half = firsts[device]
        proj_table = project_all(first_half, face_proj)
        traces = face_traces(proj_table, arrivals(strike_first, depth_first, device), device_block(neighbours, device, ELEM_DEV), device_block(face_orient, device, ELEM_DEV))
        advanced = state_block + update(first_half, proj_table, traces, jac_block, device_block(flux_local, device, ELEM_DEV), device_block(flux_neigh, device, ELEM_DEV), volume, face_lift)
        repeated = integrals(advanced, jac_block, stiffness, False)[0]
        later_half = jnp.where(device_block(cluster, device, ELEM_DEV)[None, None, :] == 0, repeated, seconds[device])
        strike_out, depth_out = sends_of(project_all(later_half, face_proj), device)
        return (advanced, later_half, strike_out, depth_out)
    advanced_all, later_all, strike_later, depth_later = lax.map(phase_two, device_ids)

    def phase_three(device):
        jac_block = device_block(jacobians, device, ELEM_DEV)
        first_table = project_all(firsts[device], face_proj)
        later_half = later_all[device]
        later_table = project_all(later_half, face_proj)
        traces = face_traces(later_table, arrivals(strike_later, depth_later, device), device_block(neighbours, device, ELEM_DEV), device_block(face_orient, device, ELEM_DEV))
        combined = advanced_all[device] + update(later_half, later_table, traces, jac_block, device_block(flux_local, device, ELEM_DEV), device_block(flux_neigh, device, ELEM_DEV), volume, face_lift)
        total_flat = (first_table + later_table).reshape(QUANT, FACE_BASIS, PROJS * ELEM_DEV)
        own_trace = jnp.take(total_flat, device_block(fault_proj, device, FAULT_DEV) * ELEM_DEV + device_block(fault_elem, device, FAULT_DEV), axis=2)
        return (combined, own_trace)
    combined_all, fault_traces = lax.map(phase_three, device_ids)

    def phase_four(device):
        partner = jnp.bitwise_xor(device, 1)
        fault_side = jnp.where(device % N_DEPTH % 2 == 0, 1.0, -1.0)
        correction = fault_correction(fault_traces[device], fault_traces[partner], fault_side, device_block(strength, device, FAULT_DEV), face_lift, device_block(fault_proj, device, FAULT_DEV), device_block(fault_elem, device, FAULT_DEV), ELEM_DEV)
        return combined_all[device] + correction
    finals = lax.map(phase_four, device_ids)
    return jnp.transpose(finals, (1, 2, 0, 3)).reshape(QUANT, BASIS, ELEMS)
```

```python
import jax
import jax.numpy as jnp
from jax import lax
from jax.experimental import pallas as pl
from jax.experimental.pallas import tpu as pltpu
from jax.sharding import PartitionSpec as P


BASIS = 56
FACE_BASIS = 21
FACE_ROWS = 24
ORDER = 6
PROJS = 12
FACES = 4
WIDE = 32
LANES = 128
TILES = 3
COEFS = 21
CHUNKS = ((0, 32), (32, 24))

fast_step = 0.5
f32 = jnp.float32
bf16 = jnp.bfloat16


def split(values):
    high = values.astype(bf16).astype(f32)
    return high, values - high


def right3(values):
    high, low = split(values)
    return jnp.concatenate([high, high, low], axis=0).astype(bf16)


def left3(weights):
    high, low = split(weights)
    return jnp.concatenate([high, low, high], axis=1).astype(bf16)


def mm(left, right):
    return jnp.dot(left, right, preferred_element_type=f32)


def stacked(tiles):
    return jnp.concatenate([right3(tile) for tile in tiles], axis=1)


def lane_tiled(row):
    return jnp.concatenate([row] * (LANES // row.shape[1]), axis=1)


def build_coefs(source, target):
    def across(pieces):
        return jnp.concatenate(pieces, axis=1)

    kinds = source.shape[2]
    for out in range(2):
        for into in range(2):
            for turn in range(4):
                target[(out * 2 + into) * 4 + turn, 0:kinds, :] = across(
                    [source[4 * out + g, 4 * into + (g - turn) % 4] for g in range(4)]
                )
        target[16 + out, 0:kinds, :] = across([source[4 * out + g, 8] for g in range(4)])
        target[18 + out, 0:kinds, :] = across([source[8, 4 * out + g] for g in range(4)])
    corner = source[8, 8]
    empty = jnp.zeros_like(corner)
    target[20, 0:kinds, :] = across([corner, empty, empty, empty])


def contract(coefs, terms):
    totals = [None, None, None]

    def add(which, kind, slot, values):
        product = coefs[slot, kind : kind + 1, :] * values
        totals[which] = product if totals[which] is None else totals[which] + product

    for kind, tiles in terms:
        for into in range(2):
            for turn in range(4):
                turned = pltpu.roll(tiles[into], WIDE * turn, 1) if turn else tiles[into]
                for out in range(2):
                    add(out, kind, (out * 2 + into) * 4 + turn, turned)
                if turn == 0:
                    add(2, kind, 18 + into, turned)
        for out in range(2):
            add(out, kind, 16 + out, tiles[2])
        add(2, kind, 20, tiles[2])
    last = totals[2]
    last = last + pltpu.roll(last, 2 * WIDE, 1)
    last = last + pltpu.roll(last, WIDE, 1)
    return totals[0], totals[1], last


def volume_like(tiles, weights3, coefs):
    applied = mm(weights3, stacked(tiles))
    pieces = []
    for start, size in CHUNKS:
        terms = []
        for d in range(3):
            rows = applied[BASIS * d + start : BASIS * d + start + size]
            terms.append((d, [rows[:, LANES * t : LANES * (t + 1)] for t in range(TILES)]))
        pieces.append(contract(coefs, terms))
    return [
        jnp.concatenate([piece[t] for piece in pieces], axis=0) for t in range(TILES)
    ]


def integrals(tiles, weights3, coefs, with_second):
    current = tiles
    first = second = None
    factorial = 1.0
    for degree in range(ORDER):
        factorial = factorial * (degree + 1)
        early = fast_step ** (degree + 1)
        late = (2.0 * fast_step) ** (degree + 1) - early
        term = [tile * (early / factorial) for tile in current]
        first = term if first is None else [a + b for a, b in zip(first, term)]
        if with_second:
            term = [tile * (late / factorial) for tile in current]
            second = term if second is None else [a + b for a, b in zip(second, term)]
        if degree + 1 < ORDER:
            current = volume_like(current, weights3, coefs)
    return first, second


def iotas(rows, columns):
    shape = (rows, columns)
    return (
        lax.broadcasted_iota(jnp.int32, shape, 0),
        lax.broadcasted_iota(jnp.int32, shape, 1),
    )


def one_hot(mask):
    return jnp.where(mask, 1.0, 0.0).astype(bf16)


def picking(elements):
    sublane, lane = iotas(LANES, LANES)
    return one_hot(sublane == elements + (lane // WIDE) * WIDE)


def traces(gathered, labels, proj3):
    count = len(gathered)
    right = jnp.concatenate(
        [jnp.concatenate([h, h, l], axis=0).astype(bf16) for h, l in gathered], axis=1
    )
    table = mm(proj3, right)
    found = []
    for i in range(count):
        column = table[:, LANES * i : LANES * (i + 1)]
        picked = column[0:FACE_ROWS]
        for m in range(1, PROJS):
            picked = jnp.where(
                labels[i] == m, column[FACE_ROWS * m : FACE_ROWS * (m + 1)], picked
            )
        found.append(picked)
    return found


def picked_traces(tiles, pickers, labels, proj3):
    parts = []
    for tile in tiles:
        parts.extend(split(tile))
    rows = jnp.concatenate(parts, axis=0).astype(bf16)
    moved = mm(rows, pickers)
    jobs = len(labels)
    gathered, marks = [], []
    for j in range(jobs):
        column = moved[:, LANES * j : LANES * (j + 1)]
        for t in range(TILES):
            at = 2 * BASIS * t
            gathered.append((column[at : at + BASIS], column[at + BASIS : at + 2 * BASIS]))
            marks.append(labels[j])
    found = traces(gathered, marks, proj3)
    return [found[TILES * j : TILES * (j + 1)] for j in range(jobs)]


def load_tiles(ref):
    return [ref[t] for t in range(TILES)]


def store_tiles(ref, tiles):
    for t in range(TILES):
        ref[t] = tiles[t]


def send_kernel(
    state,
    jacobians,
    stiffness,
    face_proj,
    strike_sends,
    strike_orient,
    depth_sends,
    depth_orient,
    base_out,
    first_out,
    second_out,
    jac_coefs,
    stiff3_out,
    proj3_out,
    pickers_out,
    labels_out,
    up_out,
    down_out,
    depth_out,
):
    build_coefs(jacobians, jac_coefs)
    stiff3 = left3(jnp.concatenate([-stiffness[d].T for d in range(3)], axis=0))
    tiles = [state[LANES * t : LANES * (t + 1), :].T for t in range(2)]
    last = state[2 * LANES : 2 * LANES + WIDE, :]
    tiles.append(jnp.concatenate([last] * 4, axis=0).T)
    store_tiles(base_out, tiles)
    first, second = integrals(tiles, stiff3, jac_coefs, True)
    store_tiles(first_out, first)
    store_tiles(second_out, second)
    margin = jnp.zeros((FACE_ROWS - FACE_BASIS, BASIS), f32)
    proj3 = left3(
        jnp.concatenate([piece for m in range(PROJS) for piece in (face_proj[m], margin)], axis=0)
    )
    stiff3_out[...] = stiff3
    proj3_out[...] = proj3

    def jobs(strike, depth):
        return [
            lane_tiled(strike[1:2, :]),
            lane_tiled(strike[0:1, :]),
            lane_tiled(jnp.concatenate([depth[1:2, :], depth[0:1, :]], axis=1)),
        ]

    pickers = jnp.concatenate(
        [picking(elements) for elements in jobs(strike_sends, depth_sends)], axis=1
    )
    labels = jobs(strike_orient, depth_orient)
    pickers_out[...] = pickers
    for j in range(3):
        labels_out[j : j + 1, :] = labels[j]
    up, down, sideways = picked_traces(first, pickers, labels, proj3)
    for t in range(TILES):
        at = FACE_ROWS * t
        up_out[at : at + FACE_ROWS, :] = up[t]
        down_out[at : at + FACE_ROWS, :] = down[t]
        depth_out[at : at + FACE_ROWS, :] = sideways[t]


def local_part(values, base, vol3, jac_coefs, own3, local_coefs, pickers, labels, proj3, outs):
    pre_out, flux_out, near_out = outs
    interior = volume_like(values, vol3, jac_coefs)
    for t in range(TILES):
        pre_out[t] = base[t] + interior[t]
    own = mm(own3, stacked(values))
    for f in range(FACES):
        at = FACE_ROWS * f
        rows = own[at : at + FACE_ROWS]
        fluxes = contract(
            local_coefs, [(f, [rows[:, LANES * t : LANES * (t + 1)] for t in range(TILES)])]
        )
        for t in range(TILES):
            flux_out[t, at : at + FACE_ROWS, :] = fluxes[t]
    near = picked_traces(values, pickers, labels, proj3)
    for f in range(FACES):
        at = FACE_ROWS * f
        for t in range(TILES):
            near_out[t, at : at + FACE_ROWS, :] = near[f][t]


def prepare_kernel(
    values,
    base,
    jac_coefs,
    proj3,
    volume,
    face_proj,
    flux_local,
    flux_neigh,
    face_lift,
    neighbours,
    face_orient,
    pre_out,
    flux_out,
    near_out,
    vol3_out,
    own3_out,
    local_coefs,
    neigh_coefs,
    pickers_out,
    labels_out,
    halo_out,
    lift3_out,
):
    vol3 = left3(jnp.concatenate([volume[d].T for d in range(3)], axis=0))
    vol3_out[...] = vol3
    margin = jnp.zeros((FACE_ROWS - FACE_BASIS, BASIS), f32)
    own3 = left3(
        jnp.concatenate([piece for f in range(FACES) for piece in (face_proj[3 * f], margin)], axis=0)
    )
    own3_out[...] = own3
    build_coefs(flux_local, local_coefs)
    build_coefs(flux_neigh, neigh_coefs)
    lift3_out[...] = left3(
        jnp.concatenate(
            [piece for f in range(FACES) for piece in (face_lift[:, f, :], margin)], axis=0
        ).T
    )
    behind = [lane_tiled(neighbours[f : f + 1, :]) for f in range(FACES)]
    labels = [lane_tiled(face_orient[f : f + 1, :]) for f in range(FACES)]
    sublane, lane = iotas(LANES, LANES)
    group = (lane // WIDE) * WIDE
    pickers = []
    for f in range(FACES):
        labels_out[f : f + 1, :] = labels[f]
        local = jnp.where(behind[f] < WIDE, behind[f], -4 * LANES)
        pickers.append(one_hot(sublane == local + group))
        for block in range(3):
            slot = behind[f] - WIDE * (block + 1)
            slot = jnp.where((slot >= 0) & (slot < WIDE), slot, -4 * LANES)
            halo_out[LANES * block : LANES * (block + 1), LANES * f : LANES * (f + 1)] = one_hot(
                sublane == slot + group
            )
    pickers = jnp.concatenate(pickers, axis=1)
    pickers_out[...] = pickers
    local_part(
        load_tiles(values),
        load_tiles(base),
        vol3,
        jac_coefs,
        own3,
        local_coefs,
        pickers,
        labels,
        proj3[...],
        (pre_out, flux_out, near_out),
    )


def again_kernel(
    values,
    base,
    jac_coefs,
    proj3,
    vol3,
    own3,
    local_coefs,
    pickers,
    labels,
    pre_out,
    flux_out,
    near_out,
):
    local_part(
        load_tiles(values),
        load_tiles(base),
        vol3[...],
        jac_coefs,
        own3[...],
        local_coefs,
        pickers[...],
        [labels[f : f + 1, :] for f in range(FACES)],
        proj3[...],
        (pre_out, flux_out, near_out),
    )


def face_terms(lower, upper, shallow, deep, halo, near, neigh_coefs, flux):
    rows = TILES * FACE_ROWS
    lane = iotas(rows, LANES)[1]
    blocks = [
        lower[...],
        upper[...],
        jnp.where(lane % WIDE < WIDE // 2, shallow[0:rows, :], deep[0:rows, :]),
    ]
    parts = [split(block) for block in blocks]
    left = jnp.concatenate(
        [
            jnp.concatenate([part[0] for part in parts], axis=1),
            jnp.concatenate([part[1] for part in parts], axis=1),
        ],
        axis=0,
    ).astype(bf16)
    moved = mm(left, halo[...])
    moved = moved[0:rows] + moved[rows : 2 * rows]
    sums = [[], [], []]
    for f in range(FACES):
        at = FACE_ROWS * f
        behind = [
            moved[FACE_ROWS * t : FACE_ROWS * (t + 1), LANES * f : LANES * (f + 1)]
            + near[t, at : at + FACE_ROWS, :]
            for t in range(TILES)
        ]
        through = contract(neigh_coefs, [(f, behind)])
        for t in range(TILES):
            sums[t].append(through[t] + flux[t, at : at + FACE_ROWS, :])
    return [jnp.concatenate(pieces, axis=0) for pieces in sums]


def lifted(pre, terms, lift3):
    lifts = mm(lift3[...], stacked(terms))
    return [pre[t] - lifts[:, LANES * t : LANES * (t + 1)] for t in range(TILES)]


def fault_pickers(fault_elem):
    sublane, lane = iotas(LANES, LANES)
    group = lane // WIDE
    source = lane_tiled(fault_elem[...]) + jnp.where(group == 1, WIDE, 3 * WIDE)
    hit = sublane == source
    return [
        one_hot(hit & (group == 0)),
        one_hot(hit & ((group == 1) | (group == 2))),
        one_hot(hit & (group == 3)),
    ]


def middle_kernel(
    lower,
    upper,
    shallow,
    deep,
    halo,
    near,
    neigh_coefs,
    flux,
    pre,
    lift3,
    first,
    second,
    cluster,
    stiff3,
    jac_coefs,
    pickers,
    labels,
    proj3,
    fault_elem,
    fault_proj,
    advanced_out,
    later_out,
    up_out,
    down_out,
    depth_out,
):
    terms = face_terms(lower, upper, shallow, deep, halo, near, neigh_coefs, flux)
    advanced = lifted(pre, terms, lift3)
    store_tiles(advanced_out, advanced)
    repeated = integrals(advanced, stiff3[...], jac_coefs, False)[0]
    is_fast = lane_tiled(cluster[...]) == 0
    later = [jnp.where(is_fast, repeated[t], second[t]) for t in range(TILES)]
    store_tiles(later_out, later)
    up, down, sideways = picked_traces(
        later, pickers[...], [labels[j : j + 1, :] for j in range(3)], proj3[...]
    )
    for t in range(TILES):
        at = FACE_ROWS * t
        up_out[at : at + FACE_ROWS, :] = up[t]
        down_out[at : at + FACE_ROWS, :] = down[t]
        depth_out[at : at + FACE_ROWS, :] = sideways[t]
    parts = []
    for t in range(TILES):
        parts.append(jnp.concatenate(split(first[t] + later[t]), axis=0))
    moved = mm(
        jnp.concatenate(parts, axis=1).astype(bf16),
        jnp.concatenate(fault_pickers(fault_elem), axis=0),
    )
    own = traces(
        [(moved[0:BASIS], moved[BASIS : 2 * BASIS])], [lane_tiled(fault_proj[...])], proj3[...]
    )[0]
    depth_out[TILES * FACE_ROWS :, :] = own


def final_kernel(
    lower,
    upper,
    shallow,
    deep,
    halo,
    near,
    neigh_coefs,
    flux,
    pre,
    lift3,
    sent,
    strength,
    fault_elem,
    fault_proj,
    even,
    result,
):
    at = TILES * FACE_ROWS
    own = sent[at:, :]
    is_even = even[0:1, :] > 0.5
    side = jnp.where(is_even, 1.0, -1.0)
    other = jnp.where(is_even, deep[at:, :], shallow[at:, :])
    group = iotas(FACE_ROWS, LANES)[1] // WIDE
    mean = 0.5 * (own + other)
    jump = side * (0.5 * (other - own))
    shear = mean + pltpu.roll(jump, 2 * WIDE, 1)
    shear = jnp.where(group < 2, shear, pltpu.roll(shear, 2 * WIDE, 1))
    square = shear * shear
    twin = jnp.where(
        group % 2 == 0, pltpu.roll(square, 3 * WIDE, 1), pltpu.roll(square, WIDE, 1)
    )
    limit = lane_tiled(strength[...])
    factor = limit / jnp.maximum(jnp.sqrt(square + twin), limit)
    traction = shear * factor
    jump = jnp.where(group < 2, traction, side * (traction - shear))
    face = lane_tiled(fault_proj[...]) // 3
    placed = jnp.concatenate([jnp.where(face == f, jump, 0.0) for f in range(FACES)], axis=0)
    spread = lax.dot_general(
        jnp.concatenate(split(placed), axis=0).astype(bf16),
        jnp.concatenate(fault_pickers(fault_elem), axis=0),
        (((1,), (1,)), ((), ())),
        preferred_element_type=f32,
    )
    rows = FACES * FACE_ROWS
    spread = spread[0:rows] + spread[rows : 2 * rows]
    terms = face_terms(lower, upper, shallow, deep, halo, near, neigh_coefs, flux)
    terms = [terms[t] - spread[:, LANES * t : LANES * (t + 1)] for t in range(TILES)]
    new = lifted(pre, terms, lift3)
    for t in range(2):
        result[LANES * t : LANES * (t + 1), :] = new[t].T
    result[2 * LANES : 2 * LANES + WIDE, :] = new[2].T[3 * WIDE : 4 * WIDE, :]


def call(kernel, name, outs, *operands):
    vmem = pl.BlockSpec(memory_space=pltpu.VMEM)
    return pl.pallas_call(
        kernel,
        out_shape=[jax.ShapeDtypeStruct(shape, dtype) for shape, dtype in outs],
        in_specs=[vmem] * len(operands),
        out_specs=[vmem] * len(outs),
        compiler_params=pltpu.CompilerParams(vmem_limit_bytes=40 * 1024 * 1024),
        name=name,
    )(*operands)


def passed_along(message, axis, by):
    length = lax.axis_size(axis)
    pairs = [(i, i + by) for i in range(length) if 0 <= i + by < length]
    return lax.ppermute(message, axis, pairs)


def exchanged(up, down, sideways):
    return (
        passed_along(up, "strike", 1),
        passed_along(down, "strike", -1),
        passed_along(sideways, "depth", 1),
        passed_along(sideways, "depth", -1),
    )


def per_device(
    state_dofs,
    jacobians,
    flux_local,
    flux_neigh,
    stiffness,
    volume,
    face_proj,
    face_lift,
    strength,
    cluster,
    neighbours,
    face_orient,
    strike_sends,
    strike_orient,
    depth_sends,
    depth_orient,
    fault_elem,
    fault_proj,
):
    quant, basis, elems = state_dofs.shape
    state = jnp.transpose(state_dofs, (0, 2, 1)).reshape(quant * elems, basis)
    jac = jnp.transpose(jacobians, (1, 2, 0, 3))
    local = jnp.transpose(flux_local, (1, 2, 0, 3))
    neigh = jnp.transpose(flux_neigh, (1, 2, 0, 3))
    proj = jnp.transpose(face_proj, (0, 2, 1))
    lift = jnp.transpose(face_lift, (1, 0, 2))
    strength, cluster, fault_elem, fault_proj = (
        array.reshape(1, -1) for array in (strength, cluster, fault_elem, fault_proj)
    )
    even = jnp.broadcast_to((1 - lax.axis_index("depth") % 2).astype(f32), (1, LANES))

    full = ((TILES, BASIS, LANES), f32)
    faces = ((TILES, FACES * FACE_ROWS, LANES), f32)
    coefs = ((COEFS, 4, LANES), f32)
    message = ((TILES * FACE_ROWS, LANES), f32)
    longer = ((TILES * FACE_ROWS + FACE_ROWS, LANES), f32)

    (
        base,
        first,
        second,
        jac_coefs,
        stiff3,
        proj3,
        pickers,
        labels,
        up,
        down,
        sideways,
    ) = call(
        send_kernel,
        "first_sends",
        [
            full,
            full,
            full,
            coefs,
            ((3 * BASIS, 3 * BASIS), bf16),
            ((PROJS * FACE_ROWS, 3 * BASIS), bf16),
            ((LANES, 3 * LANES), bf16),
            ((3, LANES), jnp.int32),
            message,
            message,
            message,
        ],
        state,
        jac,
        stiffness,
        proj,
        strike_sends,
        strike_orient,
        depth_sends,
        depth_orient,
    )
    arrived = exchanged(up, down, sideways)
    (
        pre,
        flux,
        near,
        vol3,
        own3,
        local_coefs,
        neigh_coefs,
        near_pickers,
        near_labels,
        halo,
        lift3,
    ) = call(
        prepare_kernel,
        "first_local",
        [
            full,
            faces,
            faces,
            ((3 * BASIS, 3 * BASIS), bf16),
            ((FACES * FACE_ROWS, 3 * BASIS), bf16),
            coefs,
            coefs,
            ((LANES, FACES * LANES), bf16),
            ((FACES, LANES), jnp.int32),
            ((3 * LANES, FACES * LANES), bf16),
            ((BASIS, 3 * FACES * FACE_ROWS), bf16),
        ],
        first,
        base,
        jac_coefs,
        proj3,
        volume,
        proj,
        local,
        neigh,
        lift,
        neighbours,
        face_orient,
    )
    advanced, later, up, down, sideways = call(
        middle_kernel,
        "advance",
        [full, full, message, message, longer],
        *arrived,
        halo,
        near,
        neigh_coefs,
        flux,
        pre,
        lift3,
        first,
        second,
        cluster,
        stiff3,
        jac_coefs,
        pickers,
        labels,
        proj3,
        fault_elem,
        fault_proj,
    )
    arrived = exchanged(up, down, sideways)
    pre, flux, near = call(
        again_kernel,
        "later_local",
        [full, faces, faces],
        later,
        advanced,
        jac_coefs,
        proj3,
        vol3,
        own3,
        local_coefs,
        near_pickers,
        near_labels,
    )
    (result,) = call(
        final_kernel,
        "combine",
        [((quant * elems, basis), f32)],
        *arrived,
        halo,
        near,
        neigh_coefs,
        flux,
        pre,
        lift3,
        sideways,
        strength,
        fault_elem,
        fault_proj,
        even,
    )
    return jnp.transpose(result.reshape(quant, elems, basis), (0, 2, 1))


def solution(mesh):
    spread = ("strike", "depth")
    placed = (
        P(None, None, spread),
        P(None, None, None, spread),
        P(None, None, None, spread),
        P(None, None, None, spread),
        P(),
        P(),
        P(),
        P(),
        P(spread),
        P(spread),
        P(None, spread),
        P(None, spread),
        P(None, spread),
        P(None, spread),
        P(None, spread),
        P(None, spread),
        P(spread),
        P(spread),
    )
    return jax.shard_map(
        per_device,
        mesh=mesh,
        in_specs=placed,
        out_specs=P(None, None, spread),
        check_vma=False,
    )
```

```python
import jax
import jax.numpy as jnp
from jax import lax
from jax.experimental import pallas as pl
from jax.experimental.pallas import tpu as pltpu
from jax.sharding import PartitionSpec as P


BASIS = 56
FACE_BASIS = 21
FACE_ROWS = 24
ORDER = 6
PROJS = 12
FACES = 4
WIDE = 32
LANES = 128
TILES = 3
COEFS = 21
CHUNKS = ((0, 32), (32, 24))
FAULT_ROW, CLUSTER_ROW, NEAR_ROW, ROWS = 0, 1, 2, 8

fast_step = 0.5
f32 = jnp.float32
bf16 = jnp.bfloat16


def split(values):
    high = values.astype(bf16).astype(f32)
    return high, values - high


def right3(values):
    high, low = split(values)
    return jnp.concatenate([high, high, low], axis=0).astype(bf16)


def left3(weights):
    high, low = split(weights)
    return jnp.concatenate([high, low, high], axis=1).astype(bf16)


def mm(left, right):
    return jnp.dot(left, right, preferred_element_type=f32)


def stacked(tiles):
    return jnp.concatenate([right3(tile) for tile in tiles], axis=1)


def lane_tiled(row):
    return jnp.concatenate([row] * (LANES // row.shape[1]), axis=1)


def build_coefs(source, target):
    def across(pieces):
        return jnp.concatenate(pieces, axis=1)

    kinds = source.shape[2]
    for out in range(2):
        for into in range(2):
            for turn in range(4):
                target[(out * 2 + into) * 4 + turn, 0:kinds, :] = across(
                    [source[4 * out + g, 4 * into + (g - turn) % 4] for g in range(4)]
                )
        target[16 + out, 0:kinds, :] = across([source[4 * out + g, 8] for g in range(4)])
        target[18 + out, 0:kinds, :] = across([source[8, 4 * out + g] for g in range(4)])
    corner = source[8, 8]
    empty = jnp.zeros_like(corner)
    target[20, 0:kinds, :] = across([corner, empty, empty, empty])


def contract(coefs, terms):
    totals = [None, None, None]

    def add(which, kind, slot, values):
        product = coefs[slot, kind : kind + 1, :] * values
        totals[which] = product if totals[which] is None else totals[which] + product

    for kind, tiles in terms:
        for into in range(2):
            for turn in range(4):
                turned = pltpu.roll(tiles[into], WIDE * turn, 1) if turn else tiles[into]
                for out in range(2):
                    add(out, kind, (out * 2 + into) * 4 + turn, turned)
                if turn == 0:
                    add(2, kind, 18 + into, turned)
        for out in range(2):
            add(out, kind, 16 + out, tiles[2])
        add(2, kind, 20, tiles[2])
    last = totals[2]
    last = last + pltpu.roll(last, 2 * WIDE, 1)
    last = last + pltpu.roll(last, WIDE, 1)
    return totals[0], totals[1], last


def volume_like(tiles, weights3, coefs):
    applied = mm(weights3, stacked(tiles))
    pieces = []
    for start, size in CHUNKS:
        terms = []
        for d in range(3):
            rows = applied[BASIS * d + start : BASIS * d + start + size]
            terms.append((d, [rows[:, LANES * t : LANES * (t + 1)] for t in range(TILES)]))
        pieces.append(contract(coefs, terms))
    return [
        jnp.concatenate([piece[t] for piece in pieces], axis=0) for t in range(TILES)
    ]


def integrals(tiles, weights3, coefs, with_second):
    current = tiles
    first = second = None
    factorial = 1.0
    for degree in range(ORDER):
        factorial = factorial * (degree + 1)
        early = fast_step ** (degree + 1)
        late = (2.0 * fast_step) ** (degree + 1) - early
        term = [tile * (early / factorial) for tile in current]
        first = term if first is None else [a + b for a, b in zip(first, term)]
        if with_second:
            term = [tile * (late / factorial) for tile in current]
            second = term if second is None else [a + b for a, b in zip(second, term)]
        if degree + 1 < ORDER:
            current = volume_like(current, weights3, coefs)
    return first, second


def iotas(rows, columns):
    shape = (rows, columns)
    return (
        lax.broadcasted_iota(jnp.int32, shape, 0),
        lax.broadcasted_iota(jnp.int32, shape, 1),
    )


def one_hot(mask):
    return jnp.where(mask, 1.0, 0.0).astype(bf16)


def picking(elements):
    sublane, lane = iotas(LANES, LANES)
    return one_hot(sublane == elements + (lane // WIDE) * WIDE)


def traces(gathered, labels, proj3):
    count = len(gathered)
    right = jnp.concatenate(
        [jnp.concatenate([h, h, l], axis=0).astype(bf16) for h, l in gathered], axis=1
    )
    table = mm(proj3, right)
    found = []
    for i in range(count):
        column = table[:, LANES * i : LANES * (i + 1)]
        picked = column[0:FACE_ROWS]
        for m in range(1, PROJS):
            picked = jnp.where(
                labels[i] == m, column[FACE_ROWS * m : FACE_ROWS * (m + 1)], picked
            )
        found.append(picked)
    return found


def picked_traces(tiles, pickers, labels, proj3):
    parts = []
    for tile in tiles:
        parts.extend(split(tile))
    rows = jnp.concatenate(parts, axis=0).astype(bf16)
    moved = mm(rows, pickers)
    jobs = len(labels)
    gathered, marks = [], []
    for j in range(jobs):
        column = moved[:, LANES * j : LANES * (j + 1)]
        for t in range(TILES):
            at = 2 * BASIS * t
            gathered.append((column[at : at + BASIS], column[at + BASIS : at + 2 * BASIS]))
            marks.append(labels[j])
    found = traces(gathered, marks, proj3)
    return [found[TILES * j : TILES * (j + 1)] for j in range(jobs)]


def load_tiles(ref):
    return [ref[t] for t in range(TILES)]


def store_tiles(ref, tiles):
    for t in range(TILES):
        ref[t] = tiles[t]


def weights_kernel(stiffness, stiff3_out):
    stiff3_out[...] = left3(jnp.concatenate([-stiffness[d].T for d in range(3)], axis=0))


def plan_sends(strike_sends, strike_orient, depth_sends, depth_orient, pickers_out, rows_out):
    strike_odd = lax.axis_index("strike") % 2
    depth_odd = lax.axis_index("depth") % 2

    def either(table, odd):
        twin = table[1:2, :] * (1 - odd) + table[0:1, :] * odd
        across = table[0:1, :] * (1 - odd) + table[1:2, :] * odd
        return twin, across

    def jobs(strike, depth):
        twin, across = either(strike, strike_odd)
        return [
            lane_tiled(twin),
            lane_tiled(across),
            lane_tiled(jnp.concatenate(either(depth, depth_odd), axis=1)),
        ]

    elements = jobs(strike_sends, depth_sends)
    labels = jobs(strike_orient, depth_orient)
    for j in range(3):
        pickers_out[:, LANES * j : LANES * (j + 1)] = picking(elements[j])
        rows_out[j : j + 1, :] = labels[j]


def plan_faces(neighbours, face_orient, near_pickers_out, halo_out, marks_out):
    strike_odd = lax.axis_index("strike") % 2
    depth_odd = lax.axis_index("depth") % 2
    sublane, lane = iotas(LANES, LANES)
    group = (lane // WIDE) * WIDE
    for f in range(FACES):
        behind = lane_tiled(neighbours[f : f + 1, :])
        marks_out[NEAR_ROW + f : NEAR_ROW + f + 1, :] = lane_tiled(face_orient[f : f + 1, :])
        columns = slice(LANES * f, LANES * (f + 1))
        local = jnp.where(behind < WIDE, behind, -4 * LANES)
        near_pickers_out[:, columns] = one_hot(sublane == local + group)
        strike_slot = (behind - WIDE) ^ (WIDE * (1 - strike_odd))
        depth_slot = (behind - 3 * WIDE) ^ ((WIDE // 2) * (1 - depth_odd))
        for block, slot in enumerate((strike_slot, strike_slot - WIDE, depth_slot)):
            if block < 2:
                inside = (behind >= WIDE) & (behind < 3 * WIDE)
            else:
                inside = (behind >= 3 * WIDE) & (behind < 4 * WIDE)
            inside = inside & (slot >= 0) & (slot < WIDE)
            slot = jnp.where(inside, slot, -4 * LANES)
            halo_out[LANES * block : LANES * (block + 1), columns] = one_hot(
                sublane == slot + group
            )


def send_kernel(
    state,
    jacobians,
    face_proj,
    strike_sends,
    strike_orient,
    depth_sends,
    depth_orient,
    stiff3,
    base_out,
    first_out,
    second_out,
    jac_coefs,
    proj3_out,
    pickers_out,
    rows_out,
    twin_out,
    across_out,
    depth_out,
):
    build_coefs(jacobians, jac_coefs)
    plan_sends(strike_sends, strike_orient, depth_sends, depth_orient, pickers_out, rows_out)
    tiles = [state[LANES * t : LANES * (t + 1), :].T for t in range(2)]
    last = state[2 * LANES : 2 * LANES + WIDE, :]
    tiles.append(jnp.concatenate([last] * 4, axis=0).T)
    store_tiles(base_out, tiles)
    first, second = integrals(tiles, stiff3[...], jac_coefs, True)
    store_tiles(first_out, first)
    store_tiles(second_out, second)
    margin = jnp.zeros((FACE_ROWS - FACE_BASIS, BASIS), f32)
    proj3 = left3(
        jnp.concatenate([piece for m in range(PROJS) for piece in (face_proj[m], margin)], axis=0)
    )
    proj3_out[...] = proj3
    send(first, pickers_out, rows_out, proj3, twin_out, across_out, depth_out)


def send(values, pickers, rows, proj3, *outs):
    found = picked_traces(
        values,
        pickers[...],
        [rows[j : j + 1, :] for j in range(3)],
        proj3,
    )
    for out, pieces in zip(outs, found):
        for t in range(TILES):
            out[FACE_ROWS * t : FACE_ROWS * (t + 1), :] = pieces[t]


def local_part(values, base, vol3, jac_coefs, own3, local_coefs, pickers, labels, proj3, outs):
    pre_out, flux_out, near_out = outs
    interior = volume_like(values, vol3, jac_coefs)
    for t in range(TILES):
        pre_out[t] = base[t] + interior[t]
    own = mm(own3, stacked(values))
    for f in range(FACES):
        at = FACE_ROWS * f
        rows = own[at : at + FACE_ROWS]
        fluxes = contract(
            local_coefs, [(f, [rows[:, LANES * t : LANES * (t + 1)] for t in range(TILES)])]
        )
        for t in range(TILES):
            flux_out[t, at : at + FACE_ROWS, :] = fluxes[t]
    near = picked_traces(values, pickers, labels, proj3)
    for f in range(FACES):
        at = FACE_ROWS * f
        for t in range(TILES):
            near_out[t, at : at + FACE_ROWS, :] = near[f][t]


def near_labels(marks):
    return [marks[NEAR_ROW + f : NEAR_ROW + f + 1, :] for f in range(FACES)]


def prepare_kernel(
    values,
    base,
    jac_coefs,
    proj3,
    neighbours,
    face_orient,
    volume,
    face_proj,
    flux_local,
    flux_neigh,
    face_lift,
    cluster,
    strength,
    fault_elem,
    fault_proj,
    pre_out,
    flux_out,
    near_out,
    vol3_out,
    own3_out,
    local_coefs,
    neigh_coefs,
    lift3_out,
    near_pickers_out,
    halo_out,
    fault_pickers_out,
    marks_out,
    reals_out,
):
    depth_odd = lax.axis_index("depth") % 2
    fault_pickers_out[...] = jnp.concatenate(fault_pickers(fault_elem), axis=0)
    marks_out[FAULT_ROW : FAULT_ROW + 1, :] = lane_tiled(fault_proj[...])
    marks_out[CLUSTER_ROW : CLUSTER_ROW + 1, :] = lane_tiled(cluster[...])
    reals_out[0:1, :] = lane_tiled(strength[...])
    reals_out[1:2, :] = jnp.where(iotas(1, LANES)[1] * 0 + depth_odd == 0, 1.0, -1.0)
    plan_faces(neighbours, face_orient, near_pickers_out, halo_out, marks_out)
    vol3 = left3(jnp.concatenate([volume[d].T for d in range(3)], axis=0))
    vol3_out[...] = vol3
    margin = jnp.zeros((FACE_ROWS - FACE_BASIS, BASIS), f32)
    own3 = left3(
        jnp.concatenate([piece for f in range(FACES) for piece in (face_proj[3 * f], margin)], axis=0)
    )
    own3_out[...] = own3
    build_coefs(flux_local, local_coefs)
    build_coefs(flux_neigh, neigh_coefs)
    lift3_out[...] = left3(
        jnp.concatenate(
            [piece for f in range(FACES) for piece in (face_lift[:, f, :], margin)], axis=0
        ).T
    )
    local_part(
        load_tiles(values),
        load_tiles(base),
        vol3,
        jac_coefs,
        own3,
        local_coefs,
        near_pickers_out[...],
        near_labels(marks_out),
        proj3[...],
        (pre_out, flux_out, near_out),
    )


def again_kernel(
    values,
    base,
    jac_coefs,
    proj3,
    pickers,
    marks,
    vol3,
    own3,
    local_coefs,
    pre_out,
    flux_out,
    near_out,
):
    local_part(
        load_tiles(values),
        load_tiles(base),
        vol3[...],
        jac_coefs,
        own3[...],
        local_coefs,
        pickers[...],
        near_labels(marks),
        proj3[...],
        (pre_out, flux_out, near_out),
    )


def face_terms(twin, across, pair, beyond, halo, near, neigh_coefs, flux):
    rows = TILES * FACE_ROWS
    lane = iotas(rows, LANES)[1]
    blocks = [
        twin[...],
        across[...],
        jnp.where(lane % WIDE < WIDE // 2, pair[0:rows, :], beyond[...]),
    ]
    parts = [split(block) for block in blocks]
    left = jnp.concatenate(
        [
            jnp.concatenate([part[0] for part in parts], axis=1),
            jnp.concatenate([part[1] for part in parts], axis=1),
        ],
        axis=0,
    ).astype(bf16)
    moved = mm(left, halo[...])
    moved = moved[0:rows] + moved[rows : 2 * rows]
    sums = [[], [], []]
    for f in range(FACES):
        at = FACE_ROWS * f
        behind = [
            moved[FACE_ROWS * t : FACE_ROWS * (t + 1), LANES * f : LANES * (f + 1)]
            + near[t, at : at + FACE_ROWS, :]
            for t in range(TILES)
        ]
        through = contract(neigh_coefs, [(f, behind)])
        for t in range(TILES):
            sums[t].append(through[t] + flux[t, at : at + FACE_ROWS, :])
    return [jnp.concatenate(pieces, axis=0) for pieces in sums]


def lifted(pre, terms, lift3):
    lifts = mm(lift3[...], stacked(terms))
    return [pre[t] - lifts[:, LANES * t : LANES * (t + 1)] for t in range(TILES)]


def fault_pickers(fault_elem):
    sublane, lane = iotas(LANES, LANES)
    group = lane // WIDE
    source = lane_tiled(fault_elem[...]) + jnp.where(group == 1, WIDE, 3 * WIDE)
    hit = sublane == source
    return [
        one_hot(hit & (group == 0)),
        one_hot(hit & ((group == 1) | (group == 2))),
        one_hot(hit & (group == 3)),
    ]


def middle_kernel(
    twin,
    across,
    pair,
    beyond,
    halo,
    near,
    neigh_coefs,
    flux,
    pre,
    lift3,
    first,
    second,
    stiff3,
    jac_coefs,
    pickers,
    rows,
    proj3,
    fault_picker,
    marks,
    advanced_out,
    later_out,
    twin_out,
    across_out,
    depth_out,
    pair_out,
):
    terms = face_terms(twin, across, pair, beyond, halo, near, neigh_coefs, flux)
    advanced = lifted(pre, terms, lift3)
    store_tiles(advanced_out, advanced)
    repeated = integrals(advanced, stiff3[...], jac_coefs, False)[0]
    is_fast = marks[CLUSTER_ROW : CLUSTER_ROW + 1, :] == 0
    later = [jnp.where(is_fast, repeated[t], second[t]) for t in range(TILES)]
    store_tiles(later_out, later)
    send(later, pickers, rows, proj3[...], twin_out, across_out, depth_out)
    parts = []
    for t in range(TILES):
        parts.append(jnp.concatenate(split(first[t] + later[t]), axis=0))
    moved = mm(jnp.concatenate(parts, axis=1).astype(bf16), fault_picker[...])
    own = traces(
        [(moved[0:BASIS], moved[BASIS : 2 * BASIS])],
        [marks[FAULT_ROW : FAULT_ROW + 1, :]],
        proj3[...],
    )[0]
    pair_out[0 : TILES * FACE_ROWS, :] = depth_out[...]
    pair_out[TILES * FACE_ROWS :, :] = own


def final_kernel(
    twin,
    across,
    pair,
    beyond,
    halo,
    near,
    neigh_coefs,
    flux,
    pre,
    lift3,
    sent,
    marks,
    reals,
    fault_picker,
    result,
):
    at = TILES * FACE_ROWS
    own = sent[at:, :]
    other = pair[at:, :]
    limit = reals[0:1, :]
    side = reals[1:2, :]
    group = iotas(FACE_ROWS, LANES)[1] // WIDE
    mean = 0.5 * (own + other)
    jump = side * (0.5 * (other - own))
    shear = mean + pltpu.roll(jump, 2 * WIDE, 1)
    shear = jnp.where(group < 2, shear, pltpu.roll(shear, 2 * WIDE, 1))
    square = shear * shear
    mate = jnp.where(
        group % 2 == 0, pltpu.roll(square, 3 * WIDE, 1), pltpu.roll(square, WIDE, 1)
    )
    factor = limit / jnp.maximum(jnp.sqrt(square + mate), limit)
    traction = shear * factor
    jump = jnp.where(group < 2, traction, side * (traction - shear))
    face = marks[FAULT_ROW : FAULT_ROW + 1, :] // 3
    placed = jnp.concatenate([jnp.where(face == f, jump, 0.0) for f in range(FACES)], axis=0)
    spread = lax.dot_general(
        jnp.concatenate(split(placed), axis=0).astype(bf16),
        fault_picker[...],
        (((1,), (1,)), ((), ())),
        preferred_element_type=f32,
    )
    count = FACES * FACE_ROWS
    spread = spread[0:count] + spread[count : 2 * count]
    terms = face_terms(twin, across, pair, beyond, halo, near, neigh_coefs, flux)
    terms = [terms[t] - spread[:, LANES * t : LANES * (t + 1)] for t in range(TILES)]
    new = lifted(pre, terms, lift3)
    for t in range(2):
        result[LANES * t : LANES * (t + 1), :] = new[t].T
    result[2 * LANES : 2 * LANES + WIDE, :] = new[2].T[3 * WIDE : 4 * WIDE, :]


COSTS = dict(weights=100000, first_sends=8, first_local=4, advance=8, later_local=4, combine=4)


def call(kernel, name, outs, *operands):
    vmem = pl.BlockSpec(memory_space=pltpu.VMEM)
    return pl.pallas_call(
        kernel,
        out_shape=[jax.ShapeDtypeStruct(shape, dtype) for shape, dtype in outs],
        in_specs=[vmem] * len(operands),
        out_specs=[vmem] * len(outs),
        compiler_params=pltpu.CompilerParams(vmem_limit_bytes=40 * 1024 * 1024),
        cost_estimate=pl.CostEstimate(
            flops=COSTS[name] * 10**6, bytes_accessed=COSTS[name] * 10**6, transcendentals=0
        ),
        name=name,
    )(*operands)


def with_twin(message, axis):
    length = lax.axis_size(axis)
    return lax.ppermute(message, axis, [(i, i ^ 1) for i in range(length)])


def with_other_side(message, axis):
    length = lax.axis_size(axis)
    pairs = [(i, (i - 1 ^ 1) + 1) for i in range(1, length - 1)]
    return lax.ppermute(message, axis, pairs)


def exchanged(twin, across, pair, beyond):
    pair = with_twin(pair, "depth")
    beyond = with_other_side(beyond, "depth")
    across = with_other_side(across, "strike")
    twin = with_twin(twin, "strike")
    return twin, across, pair, beyond


def per_device(
    state_dofs,
    jacobians,
    flux_local,
    flux_neigh,
    stiffness,
    volume,
    face_proj,
    face_lift,
    strength,
    cluster,
    neighbours,
    face_orient,
    strike_sends,
    strike_orient,
    depth_sends,
    depth_orient,
    fault_elem,
    fault_proj,
):
    quant, basis, elems = state_dofs.shape
    state = jnp.transpose(state_dofs, (0, 2, 1)).reshape(quant * elems, basis)
    jac = jnp.transpose(jacobians, (1, 2, 0, 3))
    local = jnp.transpose(flux_local, (1, 2, 0, 3))
    neigh = jnp.transpose(flux_neigh, (1, 2, 0, 3))
    proj = jnp.transpose(face_proj, (0, 2, 1))
    lift = jnp.transpose(face_lift, (1, 0, 2))
    strength, cluster, fault_elem, fault_proj = (
        array.reshape(1, -1) for array in (strength, cluster, fault_elem, fault_proj)
    )

    full = ((TILES, BASIS, LANES), f32)
    faces = ((TILES, FACES * FACE_ROWS, LANES), f32)
    coefs = ((COEFS, 4, LANES), f32)
    message = ((TILES * FACE_ROWS, LANES), f32)
    longer = ((TILES * FACE_ROWS + FACE_ROWS, LANES), f32)

    (stiff3,) = call(
        weights_kernel, "weights", [((3 * BASIS, 3 * BASIS), bf16)], stiffness
    )
    base, first, second, jac_coefs, proj3, pickers, rows, twin, across, sideways = call(
        send_kernel,
        "first_sends",
        [
            full,
            full,
            full,
            coefs,
            ((PROJS * FACE_ROWS, 3 * BASIS), bf16),
            ((LANES, 3 * LANES), bf16),
            ((ROWS, LANES), jnp.int32),
            message,
            message,
            message,
        ],
        state,
        jac,
        proj,
        strike_sends,
        strike_orient,
        depth_sends,
        depth_orient,
        stiff3,
    )
    arrived = exchanged(twin, across, sideways, sideways)
    pre, flux, near, vol3, own3, local_coefs, neigh_coefs, *rest = call(
        prepare_kernel,
        "first_local",
        [
            full,
            faces,
            faces,
            ((3 * BASIS, 3 * BASIS), bf16),
            ((FACES * FACE_ROWS, 3 * BASIS), bf16),
            coefs,
            coefs,
            ((BASIS, 3 * FACES * FACE_ROWS), bf16),
            ((LANES, FACES * LANES), bf16),
            ((3 * LANES, FACES * LANES), bf16),
            ((TILES * LANES, LANES), bf16),
            ((ROWS, LANES), jnp.int32),
            ((8, LANES), f32),
        ],
        first,
        base,
        jac_coefs,
        proj3,
        neighbours,
        face_orient,
        volume,
        proj,
        local,
        neigh,
        lift,
        cluster,
        strength,
        fault_elem,
        fault_proj,
    )
    lift3, near_pickers, halo, fault_picker, marks, reals = rest
    advanced, later, twin, across, sideways, pair = call(
        middle_kernel,
        "advance",
        [full, full, message, message, message, longer],
        *arrived,
        halo,
        near,
        neigh_coefs,
        flux,
        pre,
        lift3,
        first,
        second,
        stiff3,
        jac_coefs,
        pickers,
        rows,
        proj3,
        fault_picker,
        marks,
    )
    arrived = exchanged(twin, across, pair, sideways)
    pre, flux, near = call(
        again_kernel,
        "later_local",
        [full, faces, faces],
        later,
        advanced,
        jac_coefs,
        proj3,
        near_pickers,
        marks,
        vol3,
        own3,
        local_coefs,
    )
    (result,) = call(
        final_kernel,
        "combine",
        [((quant * elems, basis), f32)],
        *arrived,
        halo,
        near,
        neigh_coefs,
        flux,
        pre,
        lift3,
        pair,
        marks,
        reals,
        fault_picker,
    )
    return jnp.transpose(result.reshape(quant, elems, basis), (0, 2, 1))


def solution(mesh):
    spread = ("strike", "depth")
    placed = (
        P(None, None, spread),
        P(None, None, None, spread),
        P(None, None, None, spread),
        P(None, None, None, spread),
        P(),
        P(),
        P(),
        P(),
        P(spread),
        P(spread),
        P(None, spread),
        P(None, spread),
        P(None, spread),
        P(None, spread),
        P(None, spread),
        P(None, spread),
        P(spread),
        P(spread),
    )
    return jax.shard_map(
        per_device,
        mesh=mesh,
        in_specs=placed,
        out_specs=P(None, None, spread),
        check_vma=False,
    )
```

```python
import jax
import jax.numpy as jnp
from jax import lax
from jax.experimental import pallas as pl
from jax.experimental.pallas import tpu as pltpu
from jax.sharding import PartitionSpec as P


BASIS = 56
FACE_BASIS = 21
FACE_ROWS = 24
ORDER = 6
PROJS = 12
FACES = 4
WIDE = 32
LANES = 128
TILES = 3
COEFS = 21
FAULT_ROW, CLUSTER_ROW, ELEM_ROW, SEND_ROW, NEAR_ROW, BEHIND_ROW, ROWS = 0, 1, 2, 3, 6, 10, 16

fast_step = 0.5
f32 = jnp.float32
bf16 = jnp.bfloat16


def split(values):
    high = values.astype(bf16).astype(f32)
    return high, values - high


def right3(values):
    high, low = split(values)
    return jnp.concatenate([high, high, low], axis=0).astype(bf16)


def left3(weights):
    high, low = split(weights)
    return jnp.concatenate([high, low, high], axis=1).astype(bf16)


def mm(left, right):
    return jnp.dot(left, right, preferred_element_type=f32)


def stacked(tiles):
    return jnp.concatenate([right3(tile) for tile in tiles], axis=1)


def lane_tiled(row):
    return jnp.concatenate([row] * (LANES // row.shape[1]), axis=1)


def build_coefs(source, target):
    def across(pieces):
        return jnp.concatenate(pieces, axis=1)

    kinds = source.shape[2]
    for out in range(2):
        for into in range(2):
            for turn in range(4):
                target[(out * 2 + into) * 4 + turn, 0:kinds, :] = across(
                    [source[4 * out + (g + turn) % 4, 4 * into + g] for g in range(4)]
                )
        target[16 + out, 0:kinds, :] = across([source[4 * out + g, 8] for g in range(4)])
        target[18 + out, 0:kinds, :] = across([source[8, 4 * out + g] for g in range(4)])
    corner = source[8, 8]
    empty = jnp.zeros_like(corner)
    target[20, 0:kinds, :] = across([corner, empty, empty, empty])


def contract(coefs, terms):
    def product(slot, kind, values):
        return coefs[slot, kind : kind + 1, :] * values

    def total(products):
        result = products[0]
        for other in products[1:]:
            result = result + other
        return result

    found = []
    for out in range(2):
        sums = []
        for turn in range(4):
            products = [
                product((out * 2 + into) * 4 + turn, kind, tiles[into])
                for kind, tiles in terms
                for into in range(2)
            ]
            if turn == 0:
                products += [product(16 + out, kind, tiles[2]) for kind, tiles in terms]
            moved = total(products)
            sums.append(pltpu.roll(moved, WIDE * turn, 1) if turn else moved)
        found.append(total(sums))
    last = total(
        [product(18 + into, kind, tiles[into]) for kind, tiles in terms for into in range(2)]
        + [product(20, kind, tiles[2]) for kind, tiles in terms]
    )
    last = last + pltpu.roll(last, 2 * WIDE, 1)
    last = last + pltpu.roll(last, WIDE, 1)
    return found[0], found[1], last


def volume_like(tiles, weights3, coefs):
    whole = mm(weights3, stacked(tiles))
    applied = [whole[:, LANES * t : LANES * (t + 1)] for t in range(TILES)]
    terms = [
        (d, [part[BASIS * d : BASIS * (d + 1)] for part in applied]) for d in range(3)
    ]
    return list(contract(coefs, terms))


def integrals(tiles, weights3, coefs, with_second):
    current = tiles
    first = second = None
    factorial = 1.0
    for degree in range(ORDER):
        factorial = factorial * (degree + 1)
        early = fast_step ** (degree + 1)
        late = (2.0 * fast_step) ** (degree + 1) - early
        term = [tile * (early / factorial) for tile in current]
        first = term if first is None else [a + b for a, b in zip(first, term)]
        if with_second:
            term = [tile * (late / factorial) for tile in current]
            second = term if second is None else [a + b for a, b in zip(second, term)]
        if degree + 1 < ORDER:
            current = volume_like(current, weights3, coefs)
    return first, second


def iotas(rows, columns):
    shape = (rows, columns)
    return (
        lax.broadcasted_iota(jnp.int32, shape, 0),
        lax.broadcasted_iota(jnp.int32, shape, 1),
    )


def one_hot(mask):
    return jnp.where(mask, 1.0, 0.0).astype(bf16)


def picking(elements):
    sublane, lane = iotas(LANES, LANES)
    return one_hot(sublane == elements + (lane // WIDE) * WIDE)


def traces(gathered, labels, proj3):
    count = len(gathered)
    right = jnp.concatenate(
        [jnp.concatenate([h, h, l], axis=0).astype(bf16) for h, l in gathered], axis=1
    )
    table = mm(proj3, right)
    found = []
    for i in range(count):
        column = table[:, LANES * i : LANES * (i + 1)]
        picked = column[0:FACE_ROWS]
        for m in range(1, PROJS):
            picked = jnp.where(
                labels[i] == m, column[FACE_ROWS * m : FACE_ROWS * (m + 1)], picked
            )
        found.append(picked)
    return found


def picked_traces(tiles, pickers, labels, proj3):
    parts = []
    for tile in tiles:
        parts.extend(split(tile))
    rows = jnp.concatenate(parts, axis=0).astype(bf16)
    moved = mm(rows, pickers)
    jobs = len(labels)
    gathered, marks = [], []
    for j in range(jobs):
        column = moved[:, LANES * j : LANES * (j + 1)]
        for t in range(TILES):
            at = 2 * BASIS * t
            gathered.append((column[at : at + BASIS], column[at + BASIS : at + 2 * BASIS]))
            marks.append(labels[j])
    found = traces(gathered, marks, proj3)
    return [found[TILES * j : TILES * (j + 1)] for j in range(jobs)]


def load_tiles(ref):
    return [ref[t] for t in range(TILES)]


def store_tiles(ref, tiles):
    for t in range(TILES):
        ref[t] = tiles[t]


def either(table, axis):
    odd = lax.axis_index(axis) % 2
    twin = table[1:2, :] * (1 - odd) + table[0:1, :] * odd
    across = table[0:1, :] * (1 - odd) + table[1:2, :] * odd
    return twin, across


def plan_kernel(strike_sends, pickers_out):
    for j, elements in enumerate(either(strike_sends, "strike")):
        pickers_out[:, LANES * j : LANES * (j + 1)] = picking(lane_tiled(elements))


def plan_depth(depth_sends):
    return picking(lane_tiled(jnp.concatenate(either(depth_sends, "depth"), axis=1)))


def send_labels(strike_orient, depth_orient):
    rows = [lane_tiled(row) for row in either(strike_orient, "strike")]
    rows.append(lane_tiled(jnp.concatenate(either(depth_orient, "depth"), axis=1)))
    return rows


def plan_faces(rows, near_pickers_out, halo_out):
    strike_odd = lax.axis_index("strike") % 2
    depth_odd = lax.axis_index("depth") % 2
    sublane, lane = iotas(LANES, LANES)
    group = (lane // WIDE) * WIDE
    for f in range(FACES):
        behind = rows[BEHIND_ROW + f : BEHIND_ROW + f + 1, :]
        columns = slice(LANES * f, LANES * (f + 1))
        local = jnp.where(behind < WIDE, behind, -4 * LANES)
        near_pickers_out[:, columns] = one_hot(sublane == local + group)
        strike_slot = (behind - WIDE) ^ (WIDE * (1 - strike_odd))
        depth_slot = (behind - 3 * WIDE) ^ ((WIDE // 2) * (1 - depth_odd))
        for block, slot in enumerate((strike_slot, strike_slot - WIDE, depth_slot)):
            if block < 2:
                inside = (behind >= WIDE) & (behind < 3 * WIDE)
            else:
                inside = (behind >= 3 * WIDE) & (behind < 4 * WIDE)
            inside = inside & (slot >= 0) & (slot < WIDE)
            slot = jnp.where(inside, slot, -4 * LANES)
            halo_out[LANES * block : LANES * (block + 1), columns] = one_hot(
                sublane == slot + group
            )


def send_kernel(
    state,
    jacobians,
    stiffness,
    face_proj,
    strike_pickers,
    strike_orient,
    depth_sends,
    depth_orient,
    neighbours,
    face_orient,
    cluster,
    strength,
    fault_elem,
    fault_proj,
    base_out,
    first_out,
    second_out,
    jac_coefs,
    stiff3_out,
    proj3_out,
    pickers_out,
    rows_out,
    reals_out,
    twin_out,
    across_out,
    depth_out,
    pair_out,
):
    build_coefs(jacobians, jac_coefs)
    stiff3 = left3(jnp.concatenate([-stiffness[d].T for d in range(3)], axis=0))
    stiff3_out[...] = stiff3
    tiles = [state[LANES * t : LANES * (t + 1), :].T for t in range(2)]
    last = state[2 * LANES : 2 * LANES + WIDE, :]
    tiles.append(jnp.concatenate([last] * 4, axis=0).T)
    store_tiles(base_out, tiles)
    first, second = integrals(tiles, stiff3, jac_coefs, True)
    store_tiles(first_out, first)
    store_tiles(second_out, second)
    margin = jnp.zeros((FACE_ROWS - FACE_BASIS, BASIS), f32)
    proj3 = left3(
        jnp.concatenate([piece for m in range(PROJS) for piece in (face_proj[m], margin)], axis=0)
    )
    proj3_out[...] = proj3
    pickers_out[:, 0 : 2 * LANES] = strike_pickers[...]
    pickers_out[:, 2 * LANES : 3 * LANES] = plan_depth(depth_sends)
    for j, row in enumerate(send_labels(strike_orient, depth_orient)):
        rows_out[SEND_ROW + j : SEND_ROW + j + 1, :] = row
    send(first, pickers_out, rows_out, proj3, twin_out, across_out, depth_out, pair_out)
    rows_out[FAULT_ROW : FAULT_ROW + 1, :] = lane_tiled(fault_proj[...])
    rows_out[CLUSTER_ROW : CLUSTER_ROW + 1, :] = lane_tiled(cluster[...])
    rows_out[ELEM_ROW : ELEM_ROW + 1, :] = lane_tiled(fault_elem[...])
    for f in range(FACES):
        rows_out[NEAR_ROW + f : NEAR_ROW + f + 1, :] = lane_tiled(face_orient[f : f + 1, :])
        rows_out[BEHIND_ROW + f : BEHIND_ROW + f + 1, :] = lane_tiled(neighbours[f : f + 1, :])
    reals_out[0:1, :] = lane_tiled(strength[...])
    odd = lax.axis_index("depth") % 2
    reals_out[1:2, :] = jnp.where(iotas(1, LANES)[1] * 0 + odd == 0, 1.0, -1.0)


def send(values, pickers, rows, proj3, *outs):
    found = picked_traces(
        values,
        pickers[...],
        [rows[SEND_ROW + j : SEND_ROW + j + 1, :] for j in range(3)],
        proj3,
    )
    for out, pieces in zip(outs, (*found, found[2])):
        for t in range(TILES):
            out[FACE_ROWS * t : FACE_ROWS * (t + 1), :] = pieces[t]
        spare = out.shape[0] - TILES * FACE_ROWS
        if spare:
            out[TILES * FACE_ROWS :, :] = jnp.zeros((spare, LANES), f32)


def local_part(values, base, vol3, jac_coefs, own3, local_coefs, pickers, labels, proj3, outs):
    pre_out, flux_out, near_out = outs
    interior = volume_like(values, vol3, jac_coefs)
    for t in range(TILES):
        pre_out[t] = base[t] + interior[t]
    own = mm(own3, stacked(values))
    for f in range(FACES):
        at = FACE_ROWS * f
        rows = own[at : at + FACE_ROWS]
        fluxes = contract(
            local_coefs, [(f, [rows[:, LANES * t : LANES * (t + 1)] for t in range(TILES)])]
        )
        for t in range(TILES):
            flux_out[t, at : at + FACE_ROWS, :] = fluxes[t]
    near = picked_traces(values, pickers, labels, proj3)
    for f in range(FACES):
        at = FACE_ROWS * f
        for t in range(TILES):
            near_out[t, at : at + FACE_ROWS, :] = near[f][t]


def near_labels(rows):
    return [rows[NEAR_ROW + f : NEAR_ROW + f + 1, :] for f in range(FACES)]


def prepare_kernel(
    values,
    base,
    jac_coefs,
    proj3,
    rows,
    volume,
    face_proj,
    flux_local,
    flux_neigh,
    face_lift,
    pre_out,
    flux_out,
    near_out,
    vol3_out,
    own3_out,
    local_coefs,
    neigh_coefs,
    lift3_out,
    near_pickers_out,
    halo_out,
    fault_pickers_out,
):
    picks = fault_pickers(rows[ELEM_ROW : ELEM_ROW + 1, :])
    fault_pickers_out[...] = jnp.concatenate(picks, axis=0)
    plan_faces(rows, near_pickers_out, halo_out)
    vol3 = left3(jnp.concatenate([volume[d].T for d in range(3)], axis=0))
    vol3_out[...] = vol3
    margin = jnp.zeros((FACE_ROWS - FACE_BASIS, BASIS), f32)
    own3 = left3(
        jnp.concatenate([piece for f in range(FACES) for piece in (face_proj[3 * f], margin)], axis=0)
    )
    own3_out[...] = own3
    build_coefs(flux_local, local_coefs)
    build_coefs(flux_neigh, neigh_coefs)
    lift3_out[...] = left3(
        jnp.concatenate(
            [piece for f in range(FACES) for piece in (face_lift[:, f, :], margin)], axis=0
        ).T
    )
    local_part(
        load_tiles(values),
        load_tiles(base),
        vol3,
        jac_coefs,
        own3,
        local_coefs,
        near_pickers_out[...],
        near_labels(rows),
        proj3[...],
        (pre_out, flux_out, near_out),
    )


def again_kernel(
    values,
    base,
    jac_coefs,
    proj3,
    pickers,
    rows,
    vol3,
    own3,
    local_coefs,
    pre_out,
    flux_out,
    near_out,
):
    local_part(
        load_tiles(values),
        load_tiles(base),
        vol3[...],
        jac_coefs,
        own3[...],
        local_coefs,
        pickers[...],
        near_labels(rows),
        proj3[...],
        (pre_out, flux_out, near_out),
    )


def face_terms(twin, across, pair, beyond, halo, near, neigh_coefs, flux):
    rows = TILES * FACE_ROWS
    lane = iotas(rows, LANES)[1]
    blocks = [
        twin[...],
        across[0:rows, :],
        jnp.where(lane % WIDE < WIDE // 2, pair[0:rows, :], beyond[0:rows, :]),
    ]
    parts = [split(block) for block in blocks]
    left = jnp.concatenate(
        [
            jnp.concatenate([part[0] for part in parts], axis=1),
            jnp.concatenate([part[1] for part in parts], axis=1),
        ],
        axis=0,
    ).astype(bf16)
    moved = mm(left, halo[...])
    moved = moved[0:rows] + moved[rows : 2 * rows]
    sums = [[], [], []]
    for f in range(FACES):
        at = FACE_ROWS * f
        behind = [
            moved[FACE_ROWS * t : FACE_ROWS * (t + 1), LANES * f : LANES * (f + 1)]
            + near[t, at : at + FACE_ROWS, :]
            for t in range(TILES)
        ]
        through = contract(neigh_coefs, [(f, behind)])
        for t in range(TILES):
            sums[t].append(through[t] + flux[t, at : at + FACE_ROWS, :])
    return [jnp.concatenate(pieces, axis=0) for pieces in sums]


def lifted(pre, terms, lift3):
    lifts = mm(lift3[...], stacked(terms))
    return [pre[t] - lifts[:, LANES * t : LANES * (t + 1)] for t in range(TILES)]


def fault_pickers(fault_elem):
    sublane, lane = iotas(LANES, LANES)
    group = lane // WIDE
    source = fault_elem + jnp.where(group == 1, WIDE, 3 * WIDE)
    hit = sublane == source
    return [
        one_hot(hit & (group == 0)),
        one_hot(hit & ((group == 1) | (group == 2))),
        one_hot(hit & (group == 3)),
    ]


def middle_kernel(
    twin,
    across,
    pair,
    beyond,
    halo,
    near,
    neigh_coefs,
    flux,
    pre,
    lift3,
    first,
    second,
    stiff3,
    jac_coefs,
    pickers,
    rows,
    proj3,
    fault_picker,
    advanced_out,
    later_out,
    twin_out,
    across_out,
    depth_out,
    pair_out,
):
    terms = face_terms(twin, across, pair, beyond, halo, near, neigh_coefs, flux)
    advanced = lifted(pre, terms, lift3)
    store_tiles(advanced_out, advanced)
    repeated = integrals(advanced, stiff3[...], jac_coefs, False)[0]
    is_fast = rows[CLUSTER_ROW : CLUSTER_ROW + 1, :] == 0
    later = [jnp.where(is_fast, repeated[t], second[t]) for t in range(TILES)]
    store_tiles(later_out, later)
    send(later, pickers, rows, proj3[...], twin_out, across_out, depth_out, pair_out)
    parts = []
    for t in range(TILES):
        parts.append(jnp.concatenate(split(first[t] + later[t]), axis=0))
    moved = mm(jnp.concatenate(parts, axis=1).astype(bf16), fault_picker[...])
    own = traces(
        [(moved[0:BASIS], moved[BASIS : 2 * BASIS])],
        [rows[FAULT_ROW : FAULT_ROW + 1, :]],
        proj3[...],
    )[0]
    pair_out[TILES * FACE_ROWS : TILES * FACE_ROWS + FACE_ROWS, :] = own


def final_kernel(
    twin,
    across,
    pair,
    beyond,
    halo,
    near,
    neigh_coefs,
    flux,
    pre,
    lift3,
    sent,
    rows,
    reals,
    fault_picker,
    result,
):
    at = TILES * FACE_ROWS
    own = sent[at : at + FACE_ROWS, :]
    other = pair[at : at + FACE_ROWS, :]
    limit = reals[0:1, :]
    side = reals[1:2, :]
    group = iotas(FACE_ROWS, LANES)[1] // WIDE
    mean = 0.5 * (own + other)
    jump = side * (0.5 * (other - own))
    shear = mean + pltpu.roll(jump, 2 * WIDE, 1)
    shear = jnp.where(group < 2, shear, pltpu.roll(shear, 2 * WIDE, 1))
    square = shear * shear
    mate = jnp.where(
        group % 2 == 0, pltpu.roll(square, 3 * WIDE, 1), pltpu.roll(square, WIDE, 1)
    )
    factor = limit / jnp.maximum(jnp.sqrt(square + mate), limit)
    traction = shear * factor
    jump = jnp.where(group < 2, traction, side * (traction - shear))
    face = rows[FAULT_ROW : FAULT_ROW + 1, :] // 3
    placed = jnp.concatenate([jnp.where(face == f, jump, 0.0) for f in range(FACES)], axis=0)
    spread = lax.dot_general(
        jnp.concatenate(split(placed), axis=0).astype(bf16),
        fault_picker[...],
        (((1,), (1,)), ((), ())),
        preferred_element_type=f32,
    )
    count = FACES * FACE_ROWS
    spread = spread[0:count] + spread[count : 2 * count]
    terms = face_terms(twin, across, pair, beyond, halo, near, neigh_coefs, flux)
    terms = [terms[t] - spread[:, LANES * t : LANES * (t + 1)] for t in range(TILES)]
    new = lifted(pre, terms, lift3)
    for t in range(2):
        result[LANES * t : LANES * (t + 1), :] = new[t].T
    result[2 * LANES : 2 * LANES + WIDE, :] = new[2].T[3 * WIDE : 4 * WIDE, :]


FIRST_SPARE = (16, 8, 24)
LATER_SPARE = (16, 8, 24)
COSTS = dict(plan=100000, first_sends=100000, first_local=4, advance=8, later_local=4, combine=4)


def call(kernel, name, outs, *operands):
    vmem = pl.BlockSpec(memory_space=pltpu.VMEM)
    return pl.pallas_call(
        kernel,
        out_shape=[jax.ShapeDtypeStruct(shape, dtype) for shape, dtype in outs],
        in_specs=[vmem] * len(operands),
        out_specs=[vmem] * len(outs),
        compiler_params=pltpu.CompilerParams(vmem_limit_bytes=40 * 1024 * 1024),
        cost_estimate=pl.CostEstimate(
            flops=COSTS[name] * 10**6, bytes_accessed=COSTS[name] * 10**6, transcendentals=0
        ),
        name=name,
    )(*operands)


def with_twin(message, axis):
    length = lax.axis_size(axis)
    return lax.ppermute(message, axis, [(i, i ^ 1) for i in range(length)])


def with_other_side(message, axis):
    length = lax.axis_size(axis)
    pairs = [(i, (i - 1 ^ 1) + 1) for i in range(1, length - 1)]
    return lax.ppermute(message, axis, pairs)


def exchanged(twin, across, pair, beyond):
    pair = with_twin(pair, "depth")
    beyond = with_other_side(beyond, "depth")
    across = with_other_side(across, "strike")
    twin = with_twin(twin, "strike")
    return twin, across, pair, beyond


def per_device(
    state_dofs,
    jacobians,
    flux_local,
    flux_neigh,
    stiffness,
    volume,
    face_proj,
    face_lift,
    strength,
    cluster,
    neighbours,
    face_orient,
    strike_sends,
    strike_orient,
    depth_sends,
    depth_orient,
    fault_elem,
    fault_proj,
):
    quant, basis, elems = state_dofs.shape
    state = jnp.transpose(state_dofs, (0, 2, 1)).reshape(quant * elems, basis)
    jac = jnp.transpose(jacobians, (1, 2, 0, 3))
    local = jnp.transpose(flux_local, (1, 2, 0, 3))
    neigh = jnp.transpose(flux_neigh, (1, 2, 0, 3))
    proj = jnp.transpose(face_proj, (0, 2, 1))
    lift = jnp.transpose(face_lift, (1, 0, 2))
    strength, cluster, fault_elem, fault_proj = (
        array.reshape(1, -1) for array in (strength, cluster, fault_elem, fault_proj)
    )

    full = ((TILES, BASIS, LANES), f32)
    faces = ((TILES, FACES * FACE_ROWS, LANES), f32)
    coefs = ((COEFS, 4, LANES), f32)
    message = ((TILES * FACE_ROWS, LANES), f32)
    sized = [((TILES * FACE_ROWS + more, LANES), f32) for more in FIRST_SPARE]
    resized = [((TILES * FACE_ROWS + more, LANES), f32) for more in LATER_SPARE]

    (strike_pickers,) = call(
        plan_kernel, "plan", [((LANES, 2 * LANES), bf16)], strike_sends
    )
    base, first, second, jac_coefs, stiff3, proj3, pickers, rows, reals, *messages = call(
        send_kernel,
        "first_sends",
        [
            full,
            full,
            full,
            coefs,
            ((3 * BASIS, 3 * BASIS), bf16),
            ((PROJS * FACE_ROWS, 3 * BASIS), bf16),
            ((LANES, 3 * LANES), bf16),
            ((ROWS, LANES), jnp.int32),
            ((8, LANES), f32),
            message,
            *sized,
        ],
        state,
        jac,
        stiffness,
        proj,
        strike_pickers,
        strike_orient,
        depth_sends,
        depth_orient,
        neighbours,
        face_orient,
        cluster,
        strength,
        fault_elem,
        fault_proj,
    )
    twin, across, sideways, pair = messages
    arrived = exchanged(twin, across, pair, sideways)
    pre, flux, near, vol3, own3, local_coefs, neigh_coefs, *rest = call(
        prepare_kernel,
        "first_local",
        [
            full,
            faces,
            faces,
            ((3 * BASIS, 3 * BASIS), bf16),
            ((FACES * FACE_ROWS, 3 * BASIS), bf16),
            coefs,
            coefs,
            ((BASIS, 3 * FACES * FACE_ROWS), bf16),
            ((LANES, FACES * LANES), bf16),
            ((3 * LANES, FACES * LANES), bf16),
            ((TILES * LANES, LANES), bf16),
        ],
        first,
        base,
        jac_coefs,
        proj3,
        rows,
        volume,
        proj,
        local,
        neigh,
        lift,
    )
    lift3, near_pickers, halo, fault_picker = rest
    advanced, later, twin, across, sideways, pair = call(
        middle_kernel,
        "advance",
        [full, full, message, *resized],
        *arrived,
        halo,
        near,
        neigh_coefs,
        flux,
        pre,
        lift3,
        first,
        second,
        stiff3,
        jac_coefs,
        pickers,
        rows,
        proj3,
        fault_picker,
    )
    arrived = exchanged(twin, across, pair, sideways)
    pre, flux, near = call(
        again_kernel,
        "later_local",
        [full, faces, faces],
        later,
        advanced,
        jac_coefs,
        proj3,
        near_pickers,
        rows,
        vol3,
        own3,
        local_coefs,
    )
    (result,) = call(
        final_kernel,
        "combine",
        [((quant * elems, basis), f32)],
        *arrived,
        halo,
        near,
        neigh_coefs,
        flux,
        pre,
        lift3,
        pair,
        rows,
        reals,
        fault_picker,
    )
    return jnp.transpose(result.reshape(quant, elems, basis), (0, 2, 1))


def solution(mesh):
    spread = ("strike", "depth")
    placed = (
        P(None, None, spread),
        P(None, None, None, spread),
        P(None, None, None, spread),
        P(None, None, None, spread),
        P(),
        P(),
        P(),
        P(),
        P(spread),
        P(spread),
        P(None, spread),
        P(None, spread),
        P(None, spread),
        P(None, spread),
        P(None, spread),
        P(None, spread),
        P(spread),
        P(spread),
    )
    return jax.shard_map(
        per_device,
        mesh=mesh,
        in_specs=placed,
        out_specs=P(None, None, spread),
        check_vma=False,
    )
```

```python
import jax
import jax.numpy as jnp
from jax import lax
from jax.experimental import pallas as pl
from jax.experimental.pallas import tpu as pltpu
from jax.sharding import PartitionSpec as P


BASIS = 56
FACE_BASIS = 21
FACE_ROWS = 24
ORDER = 6
PROJS = 12
FACES = 4
WIDE = 32
LANES = 128
TILES = 3
COEFS = 21
FAULT_ROW, CLUSTER_ROW, ELEM_ROW, SEND_ROW, NEAR_ROW, BEHIND_ROW, ROWS = 0, 1, 2, 3, 6, 10, 16

fast_step = 0.5
f32 = jnp.float32
bf16 = jnp.bfloat16


def split(values):
    high = values.astype(bf16).astype(f32)
    return high, values - high


def right3(values):
    high, low = split(values)
    return jnp.concatenate([high, high, low], axis=0).astype(bf16)


def left3(weights):
    high, low = split(weights)
    return jnp.concatenate([high, low, high], axis=1).astype(bf16)


def mm(left, right):
    return jnp.dot(left, right, preferred_element_type=f32)


def stacked(tiles):
    return jnp.concatenate([right3(tile) for tile in tiles], axis=1)


def lane_tiled(row):
    return jnp.concatenate([row] * (LANES // row.shape[1]), axis=1)


def build_coefs(source, target):
    def across(pieces):
        return jnp.concatenate(pieces, axis=1)

    kinds = source.shape[2]
    for out in range(2):
        for into in range(2):
            for turn in range(4):
                target[(out * 2 + into) * 4 + turn, 0:kinds, :] = across(
                    [source[4 * out + (g + turn) % 4, 4 * into + g] for g in range(4)]
                )
        target[16 + out, 0:kinds, :] = across([source[4 * out + g, 8] for g in range(4)])
        target[18 + out, 0:kinds, :] = across([source[8, 4 * out + g] for g in range(4)])
    corner = source[8, 8]
    empty = jnp.zeros_like(corner)
    target[20, 0:kinds, :] = across([corner, empty, empty, empty])


def contract(coefs, terms):
    def product(slot, kind, values):
        return coefs[slot, kind : kind + 1, :] * values

    def total(products):
        result = products[0]
        for other in products[1:]:
            result = result + other
        return result

    found = []
    for out in range(2):
        sums = []
        for turn in range(4):
            products = [
                product((out * 2 + into) * 4 + turn, kind, tiles[into])
                for kind, tiles in terms
                for into in range(2)
            ]
            if turn == 0:
                products += [product(16 + out, kind, tiles[2]) for kind, tiles in terms]
            moved = total(products)
            sums.append(pltpu.roll(moved, WIDE * turn, 1) if turn else moved)
        found.append(total(sums))
    last = total(
        [product(18 + into, kind, tiles[into]) for kind, tiles in terms for into in range(2)]
        + [product(20, kind, tiles[2]) for kind, tiles in terms]
    )
    last = last + pltpu.roll(last, 2 * WIDE, 1)
    last = last + pltpu.roll(last, WIDE, 1)
    return found[0], found[1], last


def volume_like(tiles, weights3, coefs):
    whole = mm(weights3, stacked(tiles))
    applied = [whole[:, LANES * t : LANES * (t + 1)] for t in range(TILES)]
    terms = [
        (d, [part[BASIS * d : BASIS * (d + 1)] for part in applied]) for d in range(3)
    ]
    return list(contract(coefs, terms))


def integrals(tiles, weights3, coefs, with_second):
    current = tiles
    first = second = None
    factorial = 1.0
    for degree in range(ORDER):
        factorial = factorial * (degree + 1)
        early = fast_step ** (degree + 1)
        late = (2.0 * fast_step) ** (degree + 1) - early
        term = [tile * (early / factorial) for tile in current]
        first = term if first is None else [a + b for a, b in zip(first, term)]
        if with_second:
            term = [tile * (late / factorial) for tile in current]
            second = term if second is None else [a + b for a, b in zip(second, term)]
        if degree + 1 < ORDER:
            current = volume_like(current, weights3, coefs)
    return first, second


def iotas(rows, columns):
    shape = (rows, columns)
    return (
        lax.broadcasted_iota(jnp.int32, shape, 0),
        lax.broadcasted_iota(jnp.int32, shape, 1),
    )


def one_hot(mask):
    return jnp.where(mask, 1.0, 0.0).astype(bf16)


def picking(elements):
    sublane, lane = iotas(LANES, LANES)
    return one_hot(sublane == elements + (lane // WIDE) * WIDE)


def traces(gathered, labels, proj3):
    count = len(gathered)
    right = jnp.concatenate(
        [jnp.concatenate([h, h, l], axis=0).astype(bf16) for h, l in gathered], axis=1
    )
    table = mm(proj3, right)
    found = []
    for i in range(count):
        column = table[:, LANES * i : LANES * (i + 1)]
        picked = column[0:FACE_ROWS]
        for m in range(1, PROJS):
            picked = jnp.where(
                labels[i] == m, column[FACE_ROWS * m : FACE_ROWS * (m + 1)], picked
            )
        found.append(picked)
    return found


def picked_traces(tiles, pickers, labels, proj3, extra=None):
    parts = []
    for tile in tiles:
        parts.extend(split(tile))
    rows = jnp.concatenate(parts, axis=0).astype(bf16)
    moved = mm(rows, pickers)
    jobs = len(labels)
    gathered, marks = [], []
    for j in range(jobs):
        column = moved[:, LANES * j : LANES * (j + 1)]
        for t in range(TILES):
            at = 2 * BASIS * t
            gathered.append((column[at : at + BASIS], column[at + BASIS : at + 2 * BASIS]))
            marks.append(labels[j])
    if extra is not None:
        gathered.append(extra[0])
        marks.append(extra[1])
    found = traces(gathered, marks, proj3)
    picked = [found[TILES * j : TILES * (j + 1)] for j in range(jobs)]
    return picked if extra is None else (picked, found[-1])


def load_tiles(ref):
    return [ref[t] for t in range(TILES)]


def store_tiles(ref, tiles):
    for t in range(TILES):
        ref[t] = tiles[t]


def place_kernel(odd_out):
    lane = iotas(1, LANES)[1]
    for i, axis in enumerate(("strike", "depth")):
        odd_out[i : i + 1, :] = lane * 0 + lax.axis_index(axis) % 2


def either(table, odd):
    odd = odd[:, 0 : table.shape[1]]
    twin = table[1:2, :] * (1 - odd) + table[0:1, :] * odd
    across = table[0:1, :] * (1 - odd) + table[1:2, :] * odd
    return twin, across


def send_rows(strike, depth, odd):
    rows = [lane_tiled(row) for row in either(strike, odd[0:1, :])]
    rows.append(lane_tiled(jnp.concatenate(either(depth, odd[1:2, :]), axis=1)))
    return rows


def plan_faces(rows, near_pickers_out, halo_out):
    strike_odd = lax.axis_index("strike") % 2
    depth_odd = lax.axis_index("depth") % 2
    sublane, lane = iotas(LANES, LANES)
    group = (lane // WIDE) * WIDE
    for f in range(FACES):
        behind = rows[BEHIND_ROW + f : BEHIND_ROW + f + 1, :]
        columns = slice(LANES * f, LANES * (f + 1))
        local = jnp.where(behind < WIDE, behind, -4 * LANES)
        near_pickers_out[:, columns] = one_hot(sublane == local + group)
        strike_slot = (behind - WIDE) ^ (WIDE * (1 - strike_odd))
        depth_slot = (behind - 3 * WIDE) ^ ((WIDE // 2) * (1 - depth_odd))
        for block, slot in enumerate((strike_slot, strike_slot - WIDE, depth_slot)):
            if block < 2:
                inside = (behind >= WIDE) & (behind < 3 * WIDE)
            else:
                inside = (behind >= 3 * WIDE) & (behind < 4 * WIDE)
            inside = inside & (slot >= 0) & (slot < WIDE)
            slot = jnp.where(inside, slot, -4 * LANES)
            halo_out[LANES * block : LANES * (block + 1), columns] = one_hot(
                sublane == slot + group
            )


def send_kernel(
    state,
    jacobians,
    stiffness,
    face_proj,
    odd,
    strike_sends,
    strike_orient,
    depth_sends,
    depth_orient,
    neighbours,
    face_orient,
    cluster,
    strength,
    fault_elem,
    fault_proj,
    base_out,
    first_out,
    second_out,
    jac_coefs,
    stiff3_out,
    proj3_out,
    pickers_out,
    rows_out,
    reals_out,
    twin_out,
    across_out,
    depth_out,
    pair_out,
):
    build_coefs(jacobians, jac_coefs)
    stiff3 = left3(jnp.concatenate([-stiffness[d].T for d in range(3)], axis=0))
    stiff3_out[...] = stiff3
    tiles = [state[LANES * t : LANES * (t + 1), :].T for t in range(2)]
    last = state[2 * LANES : 2 * LANES + WIDE, :]
    tiles.append(jnp.concatenate([last] * 4, axis=0).T)
    store_tiles(base_out, tiles)
    first, second = integrals(tiles, stiff3, jac_coefs, True)
    store_tiles(first_out, first)
    store_tiles(second_out, second)
    margin = jnp.zeros((FACE_ROWS - FACE_BASIS, BASIS), f32)
    proj3 = left3(
        jnp.concatenate([piece for m in range(PROJS) for piece in (face_proj[m], margin)], axis=0)
    )
    proj3_out[...] = proj3
    for j, row in enumerate(send_rows(strike_sends, depth_sends, odd[...])):
        pickers_out[:, LANES * j : LANES * (j + 1)] = picking(row)
    for j, row in enumerate(send_rows(strike_orient, depth_orient, odd[...])):
        rows_out[SEND_ROW + j : SEND_ROW + j + 1, :] = row
    send(first, pickers_out, rows_out, proj3, (twin_out, across_out, depth_out, pair_out))
    rows_out[FAULT_ROW : FAULT_ROW + 1, :] = lane_tiled(fault_proj[...])
    rows_out[CLUSTER_ROW : CLUSTER_ROW + 1, :] = lane_tiled(cluster[...])
    rows_out[ELEM_ROW : ELEM_ROW + 1, :] = lane_tiled(fault_elem[...])
    for f in range(FACES):
        rows_out[NEAR_ROW + f : NEAR_ROW + f + 1, :] = lane_tiled(face_orient[f : f + 1, :])
        rows_out[BEHIND_ROW + f : BEHIND_ROW + f + 1, :] = lane_tiled(neighbours[f : f + 1, :])
    reals_out[0:1, :] = lane_tiled(strength[...])
    reals_out[1:2, :] = jnp.where(odd[1:2, :] == 0, 1.0, -1.0)


def send(values, pickers, rows, proj3, outs, extra=None):
    labels = [rows[SEND_ROW + j : SEND_ROW + j + 1, :] for j in range(3)]
    found = picked_traces(values, pickers[...], labels, proj3, extra)
    if extra is not None:
        found, own = found
    for out, pieces in zip(outs, (*found, found[2])):
        for t in range(TILES):
            out[FACE_ROWS * t : FACE_ROWS * (t + 1), :] = pieces[t]
        spare = out.shape[0] - TILES * FACE_ROWS
        if spare:
            out[TILES * FACE_ROWS :, :] = jnp.zeros((spare, LANES), f32)
    if extra is not None:
        outs[3][TILES * FACE_ROWS : TILES * FACE_ROWS + FACE_ROWS, :] = own


def local_part(values, base, vol3, jac_coefs, own3, local_coefs, pickers, labels, proj3, outs):
    pre_out, flux_out, near_out = outs
    interior = volume_like(values, vol3, jac_coefs)
    for t in range(TILES):
        pre_out[t] = base[t] + interior[t]
    own = mm(own3, stacked(values))
    for f in range(FACES):
        at = FACE_ROWS * f
        rows = own[at : at + FACE_ROWS]
        fluxes = contract(
            local_coefs, [(f, [rows[:, LANES * t : LANES * (t + 1)] for t in range(TILES)])]
        )
        for t in range(TILES):
            flux_out[t, at : at + FACE_ROWS, :] = fluxes[t]
    near = picked_traces(values, pickers, labels, proj3)
    for f in range(FACES):
        at = FACE_ROWS * f
        for t in range(TILES):
            near_out[t, at : at + FACE_ROWS, :] = near[f][t]


def near_labels(rows):
    return [rows[NEAR_ROW + f : NEAR_ROW + f + 1, :] for f in range(FACES)]


def prepare_kernel(
    values,
    base,
    jac_coefs,
    proj3,
    rows,
    volume,
    face_proj,
    flux_local,
    flux_neigh,
    face_lift,
    pre_out,
    flux_out,
    near_out,
    vol3_out,
    own3_out,
    local_coefs,
    neigh_coefs,
    lift3_out,
    near_pickers_out,
    halo_out,
    fault_pickers_out,
):
    picks = fault_pickers(rows[ELEM_ROW : ELEM_ROW + 1, :])
    fault_pickers_out[...] = jnp.concatenate(picks, axis=0)
    plan_faces(rows, near_pickers_out, halo_out)
    vol3 = left3(jnp.concatenate([volume[d].T for d in range(3)], axis=0))
    vol3_out[...] = vol3
    margin = jnp.zeros((FACE_ROWS - FACE_BASIS, BASIS), f32)
    own3 = left3(
        jnp.concatenate([piece for f in range(FACES) for piece in (face_proj[3 * f], margin)], axis=0)
    )
    own3_out[...] = own3
    build_coefs(flux_local, local_coefs)
    build_coefs(flux_neigh, neigh_coefs)
    lift3_out[...] = left3(
        jnp.concatenate(
            [piece for f in range(FACES) for piece in (face_lift[:, f, :], margin)], axis=0
        ).T
    )
    local_part(
        load_tiles(values),
        load_tiles(base),
        vol3,
        jac_coefs,
        own3,
        local_coefs,
        near_pickers_out[...],
        near_labels(rows),
        proj3[...],
        (pre_out, flux_out, near_out),
    )


def again_kernel(
    values,
    base,
    jac_coefs,
    proj3,
    pickers,
    rows,
    vol3,
    own3,
    local_coefs,
    pre_out,
    flux_out,
    near_out,
):
    local_part(
        load_tiles(values),
        load_tiles(base),
        vol3[...],
        jac_coefs,
        own3[...],
        local_coefs,
        pickers[...],
        near_labels(rows),
        proj3[...],
        (pre_out, flux_out, near_out),
    )


def face_terms(twin, across, pair, beyond, halo, near, neigh_coefs, flux):
    rows = TILES * FACE_ROWS
    lane = iotas(rows, LANES)[1]
    blocks = [
        twin[...],
        across[0:rows, :],
        jnp.where(lane % WIDE < WIDE // 2, pair[0:rows, :], beyond[0:rows, :]),
    ]
    parts = [split(block) for block in blocks]
    left = jnp.concatenate(
        [
            jnp.concatenate([part[0] for part in parts], axis=1),
            jnp.concatenate([part[1] for part in parts], axis=1),
        ],
        axis=0,
    ).astype(bf16)
    moved = mm(left, halo[...])
    moved = moved[0:rows] + moved[rows : 2 * rows]
    sums = [[], [], []]
    for f in range(FACES):
        at = FACE_ROWS * f
        behind = [
            moved[FACE_ROWS * t : FACE_ROWS * (t + 1), LANES * f : LANES * (f + 1)]
            + near[t, at : at + FACE_ROWS, :]
            for t in range(TILES)
        ]
        through = contract(neigh_coefs, [(f, behind)])
        for t in range(TILES):
            sums[t].append(through[t] + flux[t, at : at + FACE_ROWS, :])
    return [jnp.concatenate(pieces, axis=0) for pieces in sums]


def lifted(pre, terms, lift3):
    lifts = mm(lift3[...], stacked(terms))
    return [pre[t] - lifts[:, LANES * t : LANES * (t + 1)] for t in range(TILES)]


def fault_pickers(fault_elem):
    sublane, lane = iotas(LANES, LANES)
    group = lane // WIDE
    source = fault_elem + jnp.where(group == 1, WIDE, 3 * WIDE)
    hit = sublane == source
    return [
        one_hot(hit & (group == 0)),
        one_hot(hit & ((group == 1) | (group == 2))),
        one_hot(hit & (group == 3)),
    ]


def middle_kernel(
    twin,
    across,
    pair,
    beyond,
    halo,
    near,
    neigh_coefs,
    flux,
    pre,
    lift3,
    first,
    second,
    stiff3,
    jac_coefs,
    pickers,
    rows,
    proj3,
    fault_picker,
    advanced_out,
    later_out,
    twin_out,
    across_out,
    depth_out,
    pair_out,
):
    terms = face_terms(twin, across, pair, beyond, halo, near, neigh_coefs, flux)
    advanced = lifted(pre, terms, lift3)
    store_tiles(advanced_out, advanced)
    repeated = integrals(advanced, stiff3[...], jac_coefs, False)[0]
    is_fast = rows[CLUSTER_ROW : CLUSTER_ROW + 1, :] == 0
    later = [jnp.where(is_fast, repeated[t], second[t]) for t in range(TILES)]
    store_tiles(later_out, later)
    parts = []
    for t in range(TILES):
        parts.append(jnp.concatenate(split(first[t] + later[t]), axis=0))
    moved = mm(jnp.concatenate(parts, axis=1).astype(bf16), fault_picker[...])
    fault = (moved[0:BASIS], moved[BASIS : 2 * BASIS]), rows[FAULT_ROW : FAULT_ROW + 1, :]
    outs = (twin_out, across_out, depth_out, pair_out)
    send(later, pickers, rows, proj3[...], outs, fault)


def final_kernel(
    twin,
    across,
    pair,
    beyond,
    halo,
    near,
    neigh_coefs,
    flux,
    pre,
    lift3,
    sent,
    rows,
    reals,
    fault_picker,
    result,
):
    at = TILES * FACE_ROWS
    own = sent[at : at + FACE_ROWS, :]
    other = pair[at : at + FACE_ROWS, :]
    limit = reals[0:1, :]
    side = reals[1:2, :]
    group = iotas(FACE_ROWS, LANES)[1] // WIDE
    mean = 0.5 * (own + other)
    jump = side * (0.5 * (other - own))
    shear = mean + pltpu.roll(jump, 2 * WIDE, 1)
    shear = jnp.where(group < 2, shear, pltpu.roll(shear, 2 * WIDE, 1))
    square = shear * shear
    mate = jnp.where(
        group % 2 == 0, pltpu.roll(square, 3 * WIDE, 1), pltpu.roll(square, WIDE, 1)
    )
    factor = limit / jnp.maximum(jnp.sqrt(square + mate), limit)
    traction = shear * factor
    jump = jnp.where(group < 2, traction, side * (traction - shear))
    face = rows[FAULT_ROW : FAULT_ROW + 1, :] // 3
    placed = jnp.concatenate([jnp.where(face == f, jump, 0.0) for f in range(FACES)], axis=0)
    spread = lax.dot_general(
        jnp.concatenate(split(placed), axis=0).astype(bf16),
        fault_picker[...],
        (((1,), (1,)), ((), ())),
        preferred_element_type=f32,
    )
    count = FACES * FACE_ROWS
    spread = spread[0:count] + spread[count : 2 * count]
    terms = face_terms(twin, across, pair, beyond, halo, near, neigh_coefs, flux)
    terms = [terms[t] - spread[:, LANES * t : LANES * (t + 1)] for t in range(TILES)]
    new = lifted(pre, terms, lift3)
    for t in range(2):
        result[LANES * t : LANES * (t + 1), :] = new[t].T
    result[2 * LANES : 2 * LANES + WIDE, :] = new[2].T[3 * WIDE : 4 * WIDE, :]


FIRST_SPARE = (16, 8, 24)
LATER_SPARE = (16, 8, 24)
COSTS = dict(place=100000, first_sends=100000, first_local=4, advance=8, later_local=4, combine=4)


def call(kernel, name, outs, *operands):
    vmem = pl.BlockSpec(memory_space=pltpu.VMEM)
    return pl.pallas_call(
        kernel,
        out_shape=[jax.ShapeDtypeStruct(shape, dtype) for shape, dtype in outs],
        in_specs=[vmem] * len(operands),
        out_specs=[vmem] * len(outs),
        compiler_params=pltpu.CompilerParams(vmem_limit_bytes=40 * 1024 * 1024),
        cost_estimate=pl.CostEstimate(
            flops=COSTS[name] * 10**6, bytes_accessed=COSTS[name] * 10**6, transcendentals=0
        ),
        name=name,
    )(*operands)


def with_twin(message, axis):
    length = lax.axis_size(axis)
    return lax.ppermute(message, axis, [(i, i ^ 1) for i in range(length)])


def with_other_side(message, axis):
    length = lax.axis_size(axis)
    pairs = [(i, (i - 1 ^ 1) + 1) for i in range(1, length - 1)]
    return lax.ppermute(message, axis, pairs)


def exchanged(twin, across, pair, beyond):
    pair = with_twin(pair, "depth")
    beyond = with_other_side(beyond, "depth")
    across = with_other_side(across, "strike")
    twin = with_twin(twin, "strike")
    return twin, across, pair, beyond


def per_device(
    state_dofs,
    jacobians,
    flux_local,
    flux_neigh,
    stiffness,
    volume,
    face_proj,
    face_lift,
    strength,
    cluster,
    neighbours,
    face_orient,
    strike_sends,
    strike_orient,
    depth_sends,
    depth_orient,
    fault_elem,
    fault_proj,
):
    quant, basis, elems = state_dofs.shape
    state = jnp.transpose(state_dofs, (0, 2, 1)).reshape(quant * elems, basis)
    jac = jnp.transpose(jacobians, (1, 2, 0, 3))
    local = jnp.transpose(flux_local, (1, 2, 0, 3))
    neigh = jnp.transpose(flux_neigh, (1, 2, 0, 3))
    proj = jnp.transpose(face_proj, (0, 2, 1))
    lift = jnp.transpose(face_lift, (1, 0, 2))
    strength, cluster, fault_elem, fault_proj = (
        array.reshape(1, -1) for array in (strength, cluster, fault_elem, fault_proj)
    )

    full = ((TILES, BASIS, LANES), f32)
    faces = ((TILES, FACES * FACE_ROWS, LANES), f32)
    coefs = ((COEFS, 4, LANES), f32)
    message = ((TILES * FACE_ROWS, LANES), f32)
    sized = [((TILES * FACE_ROWS + more, LANES), f32) for more in FIRST_SPARE]
    resized = [((TILES * FACE_ROWS + more, LANES), f32) for more in LATER_SPARE]

    (odd,) = call(place_kernel, "place", [((8, LANES), jnp.int32)])
    base, first, second, jac_coefs, stiff3, proj3, pickers, rows, reals, *messages = call(
        send_kernel,
        "first_sends",
        [
            full,
            full,
            full,
            coefs,
            ((3 * BASIS, 3 * BASIS), bf16),
            ((PROJS * FACE_ROWS, 3 * BASIS), bf16),
            ((LANES, 3 * LANES), bf16),
            ((ROWS, LANES), jnp.int32),
            ((8, LANES), f32),
            message,
            *sized,
        ],
        state,
        jac,
        stiffness,
        proj,
        odd,
        strike_sends,
        strike_orient,
        depth_sends,
        depth_orient,
        neighbours,
        face_orient,
        cluster,
        strength,
        fault_elem,
        fault_proj,
    )
    twin, across, sideways, pair = messages
    arrived = exchanged(twin, across, pair, sideways)
    pre, flux, near, vol3, own3, local_coefs, neigh_coefs, *rest = call(
        prepare_kernel,
        "first_local",
        [
            full,
            faces,
            faces,
            ((3 * BASIS, 3 * BASIS), bf16),
            ((FACES * FACE_ROWS, 3 * BASIS), bf16),
            coefs,
            coefs,
            ((BASIS, 3 * FACES * FACE_ROWS), bf16),
            ((LANES, FACES * LANES), bf16),
            ((3 * LANES, FACES * LANES), bf16),
            ((TILES * LANES, LANES), bf16),
        ],
        first,
        base,
        jac_coefs,
        proj3,
        rows,
        volume,
        proj,
        local,
        neigh,
        lift,
    )
    lift3, near_pickers, halo, fault_picker = rest
    advanced, later, twin, across, sideways, pair = call(
        middle_kernel,
        "advance",
        [full, full, message, *resized],
        *arrived,
        halo,
        near,
        neigh_coefs,
        flux,
        pre,
        lift3,
        first,
        second,
        stiff3,
        jac_coefs,
        pickers,
        rows,
        proj3,
        fault_picker,
    )
    arrived = exchanged(twin, across, pair, sideways)
    pre, flux, near = call(
        again_kernel,
        "later_local",
        [full, faces, faces],
        later,
        advanced,
        jac_coefs,
        proj3,
        near_pickers,
        rows,
        vol3,
        own3,
        local_coefs,
    )
    (result,) = call(
        final_kernel,
        "combine",
        [((quant * elems, basis), f32)],
        *arrived,
        halo,
        near,
        neigh_coefs,
        flux,
        pre,
        lift3,
        pair,
        rows,
        reals,
        fault_picker,
    )
    return jnp.transpose(result.reshape(quant, elems, basis), (0, 2, 1))


def solution(mesh):
    spread = ("strike", "depth")
    placed = (
        P(None, None, spread),
        P(None, None, None, spread),
        P(None, None, None, spread),
        P(None, None, None, spread),
        P(),
        P(),
        P(),
        P(),
        P(spread),
        P(spread),
        P(None, spread),
        P(None, spread),
        P(None, spread),
        P(None, spread),
        P(None, spread),
        P(None, spread),
        P(spread),
        P(spread),
    )
    return jax.shard_map(
        per_device,
        mesh=mesh,
        in_specs=placed,
        out_specs=P(None, None, spread),
        check_vma=False,
    )
```

```python
import jax
import jax.numpy as jnp
from jax import lax
from jax.experimental import pallas as pl
from jax.experimental.pallas import tpu as pltpu
from jax.sharding import PartitionSpec as P


BASIS = 56
FACE_BASIS = 21
FACE_ROWS = 24
ORDER = 6
PROJS = 12
FACES = 4
WIDE = 32
LANES = 128
TILES = 3
COEFS = 21
FAULT_ROW, CLUSTER_ROW, ELEM_ROW, SEND_ROW, NEAR_ROW, BEHIND_ROW, ROWS = 0, 1, 2, 3, 6, 10, 16

fast_step = 0.5
f32 = jnp.float32
bf16 = jnp.bfloat16


def split(values):
    high = values.astype(bf16).astype(f32)
    return high, values - high


def right3(values):
    high, low = split(values)
    return jnp.concatenate([high, high, low], axis=0).astype(bf16)


def left3(weights):
    high, low = split(weights)
    return jnp.concatenate([high, low, high], axis=1).astype(bf16)


def mm(left, right):
    return jnp.dot(left, right, preferred_element_type=f32)


def stacked(tiles):
    return jnp.concatenate([right3(tile) for tile in tiles], axis=1)


def lane_tiled(row):
    return jnp.concatenate([row] * (LANES // row.shape[1]), axis=1)


def build_coefs(source, target):
    def across(pieces):
        return jnp.concatenate(pieces, axis=1)

    kinds = source.shape[2]
    for out in range(2):
        for into in range(2):
            for turn in range(4):
                target[(out * 2 + into) * 4 + turn, 0:kinds, :] = across(
                    [source[4 * out + (g + turn) % 4, 4 * into + g] for g in range(4)]
                )
        target[16 + out, 0:kinds, :] = across([source[4 * out + g, 8] for g in range(4)])
        target[18 + out, 0:kinds, :] = across([source[8, 4 * out + g] for g in range(4)])
    corner = source[8, 8]
    empty = jnp.zeros_like(corner)
    target[20, 0:kinds, :] = across([corner, empty, empty, empty])


def contract(coefs, terms):
    def product(slot, kind, values):
        return coefs[slot, kind : kind + 1, :] * values

    def total(products):
        result = products[0]
        for other in products[1:]:
            result = result + other
        return result

    found = []
    for out in range(2):
        sums = []
        for turn in range(4):
            products = [
                product((out * 2 + into) * 4 + turn, kind, tiles[into])
                for kind, tiles in terms
                for into in range(2)
            ]
            if turn == 0:
                products += [product(16 + out, kind, tiles[2]) for kind, tiles in terms]
            moved = total(products)
            sums.append(pltpu.roll(moved, WIDE * turn, 1) if turn else moved)
        found.append(total(sums))
    last = total(
        [product(18 + into, kind, tiles[into]) for kind, tiles in terms for into in range(2)]
        + [product(20, kind, tiles[2]) for kind, tiles in terms]
    )
    last = last + pltpu.roll(last, 2 * WIDE, 1)
    last = last + pltpu.roll(last, WIDE, 1)
    return found[0], found[1], last


def by_lanes(product):
    return [product[:, LANES * t : LANES * (t + 1)] for t in range(TILES)]


def volume_terms(product, coefs):
    applied = by_lanes(product)
    terms = [
        (d, [part[BASIS * d : BASIS * (d + 1)] for part in applied]) for d in range(3)
    ]
    return list(contract(coefs, terms))


def volume_like(tiles, weights3, coefs):
    return volume_terms(mm(weights3, stacked(tiles)), coefs)


def integrals(tiles, weights3, coefs, with_second):
    current = tiles
    first = second = None
    factorial = 1.0
    for degree in range(ORDER):
        factorial = factorial * (degree + 1)
        early = fast_step ** (degree + 1)
        late = (2.0 * fast_step) ** (degree + 1) - early
        term = [tile * (early / factorial) for tile in current]
        first = term if first is None else [a + b for a, b in zip(first, term)]
        if with_second:
            term = [tile * (late / factorial) for tile in current]
            second = term if second is None else [a + b for a, b in zip(second, term)]
        if degree + 1 < ORDER:
            current = volume_like(current, weights3, coefs)
    return first, second


def iotas(rows, columns):
    shape = (rows, columns)
    return (
        lax.broadcasted_iota(jnp.int32, shape, 0),
        lax.broadcasted_iota(jnp.int32, shape, 1),
    )


def one_hot(mask):
    return jnp.where(mask, 1.0, 0.0).astype(bf16)


def picking(elements):
    sublane, lane = iotas(LANES, LANES)
    return one_hot(sublane == elements + (lane // WIDE) * WIDE)


def traces(gathered, labels, proj3):
    count = len(gathered)
    right = jnp.concatenate(
        [jnp.concatenate([h, h, l], axis=0).astype(bf16) for h, l in gathered], axis=1
    )
    table = mm(proj3, right)
    found = []
    for i in range(count):
        column = table[:, LANES * i : LANES * (i + 1)]
        picked = column[0:FACE_ROWS]
        for m in range(1, PROJS):
            picked = jnp.where(
                labels[i] == m, column[FACE_ROWS * m : FACE_ROWS * (m + 1)], picked
            )
        found.append(picked)
    return found


def picked_traces(tiles, pickers, labels, proj3, extra=None):
    parts = []
    for tile in tiles:
        parts.extend(split(tile))
    rows = jnp.concatenate(parts, axis=0).astype(bf16)
    moved = mm(rows, pickers)
    jobs = len(labels)
    gathered, marks = [], []
    for j in range(jobs):
        column = moved[:, LANES * j : LANES * (j + 1)]
        for t in range(TILES):
            at = 2 * BASIS * t
            gathered.append((column[at : at + BASIS], column[at + BASIS : at + 2 * BASIS]))
            marks.append(labels[j])
    if extra is not None:
        gathered.append(extra[0])
        marks.append(extra[1])
    found = traces(gathered, marks, proj3)
    picked = [found[TILES * j : TILES * (j + 1)] for j in range(jobs)]
    return picked if extra is None else (picked, found[-1])


def load_tiles(ref):
    return [ref[t] for t in range(TILES)]


def store_tiles(ref, tiles):
    for t in range(TILES):
        ref[t] = tiles[t]


def place_kernel(odd_out):
    lane = iotas(1, LANES)[1]
    for i, axis in enumerate(("strike", "depth")):
        odd_out[i : i + 1, :] = lane * 0 + lax.axis_index(axis) % 2


def either(table, odd):
    odd = odd[:, 0 : table.shape[1]]
    twin = table[1:2, :] * (1 - odd) + table[0:1, :] * odd
    across = table[0:1, :] * (1 - odd) + table[1:2, :] * odd
    return twin, across


def send_rows(strike, depth, odd):
    rows = [lane_tiled(row) for row in either(strike, odd[0:1, :])]
    rows.append(lane_tiled(jnp.concatenate(either(depth, odd[1:2, :]), axis=1)))
    return rows


def plan_faces(rows, near_pickers_out, halo_out):
    strike_odd = lax.axis_index("strike") % 2
    depth_odd = lax.axis_index("depth") % 2
    sublane, lane = iotas(LANES, LANES)
    group = (lane // WIDE) * WIDE
    for f in range(FACES):
        behind = rows[BEHIND_ROW + f : BEHIND_ROW + f + 1, :]
        columns = slice(LANES * f, LANES * (f + 1))
        local = jnp.where(behind < WIDE, behind, -4 * LANES)
        near_pickers_out[:, columns] = one_hot(sublane == local + group)
        strike_slot = (behind - WIDE) ^ (WIDE * (1 - strike_odd))
        depth_slot = (behind - 3 * WIDE) ^ ((WIDE // 2) * (1 - depth_odd))
        for block, slot in enumerate((strike_slot, strike_slot - WIDE, depth_slot)):
            if block < 2:
                inside = (behind >= WIDE) & (behind < 3 * WIDE)
            else:
                inside = (behind >= 3 * WIDE) & (behind < 4 * WIDE)
            inside = inside & (slot >= 0) & (slot < WIDE)
            slot = jnp.where(inside, slot, -4 * LANES)
            halo_out[LANES * block : LANES * (block + 1), columns] = one_hot(
                sublane == slot + group
            )


def send_kernel(
    state,
    jacobians,
    stiffness,
    face_proj,
    odd,
    strike_sends,
    strike_orient,
    depth_sends,
    depth_orient,
    neighbours,
    face_orient,
    cluster,
    strength,
    fault_elem,
    fault_proj,
    base_out,
    first_out,
    second_out,
    jac_coefs,
    stiff3_out,
    proj3_out,
    pickers_out,
    rows_out,
    reals_out,
    twin_out,
    across_out,
    depth_out,
    pair_out,
):
    build_coefs(jacobians, jac_coefs)
    stiff3 = left3(jnp.concatenate([-stiffness[d].T for d in range(3)], axis=0))
    stiff3_out[...] = stiff3
    tiles = [state[LANES * t : LANES * (t + 1), :].T for t in range(2)]
    last = state[2 * LANES : 2 * LANES + WIDE, :]
    tiles.append(jnp.concatenate([last] * 4, axis=0).T)
    store_tiles(base_out, tiles)
    first, second = integrals(tiles, stiff3, jac_coefs, True)
    store_tiles(first_out, first)
    store_tiles(second_out, second)
    margin = jnp.zeros((FACE_ROWS - FACE_BASIS, BASIS), f32)
    proj3 = left3(
        jnp.concatenate([piece for m in range(PROJS) for piece in (face_proj[m], margin)], axis=0)
    )
    proj3_out[...] = proj3
    for j, row in enumerate(send_rows(strike_sends, depth_sends, odd[...])):
        pickers_out[:, LANES * j : LANES * (j + 1)] = picking(row)
    for j, row in enumerate(send_rows(strike_orient, depth_orient, odd[...])):
        rows_out[SEND_ROW + j : SEND_ROW + j + 1, :] = row
    send(first, pickers_out, rows_out, proj3, (twin_out, across_out, depth_out, pair_out))
    rows_out[FAULT_ROW : FAULT_ROW + 1, :] = lane_tiled(fault_proj[...])
    rows_out[CLUSTER_ROW : CLUSTER_ROW + 1, :] = lane_tiled(cluster[...])
    rows_out[ELEM_ROW : ELEM_ROW + 1, :] = lane_tiled(fault_elem[...])
    for f in range(FACES):
        rows_out[NEAR_ROW + f : NEAR_ROW + f + 1, :] = lane_tiled(face_orient[f : f + 1, :])
        rows_out[BEHIND_ROW + f : BEHIND_ROW + f + 1, :] = lane_tiled(neighbours[f : f + 1, :])
    reals_out[0:1, :] = lane_tiled(strength[...])
    reals_out[1:2, :] = jnp.where(odd[1:2, :] == 0, 1.0, -1.0)


def send(values, pickers, rows, proj3, outs, extra=None):
    labels = [rows[SEND_ROW + j : SEND_ROW + j + 1, :] for j in range(3)]
    found = picked_traces(values, pickers[...], labels, proj3, extra)
    if extra is not None:
        found, own = found
    for out, pieces in zip(outs, (*found, found[2])):
        for t in range(TILES):
            out[FACE_ROWS * t : FACE_ROWS * (t + 1), :] = pieces[t]
        spare = out.shape[0] - TILES * FACE_ROWS
        if spare:
            out[TILES * FACE_ROWS :, :] = jnp.zeros((spare, LANES), f32)
    if extra is not None:
        outs[3][TILES * FACE_ROWS : TILES * FACE_ROWS + FACE_ROWS, :] = own


def local_part(values, base, inner3, jac_coefs, local_coefs, pickers, labels, proj3, outs):
    pre_out, flux_out, near_out = outs
    product = mm(inner3, stacked(values))
    interior = volume_terms(product, jac_coefs)
    for t in range(TILES):
        pre_out[t] = base[t] + interior[t]
    for f in range(FACES):
        at = FACE_ROWS * f
        rows = product[3 * BASIS + at : 3 * BASIS + at + FACE_ROWS]
        fluxes = contract(
            local_coefs, [(f, by_lanes(rows))]
        )
        for t in range(TILES):
            flux_out[t, at : at + FACE_ROWS, :] = fluxes[t]
    near = picked_traces(values, pickers, labels, proj3)
    for f in range(FACES):
        at = FACE_ROWS * f
        for t in range(TILES):
            near_out[t, at : at + FACE_ROWS, :] = near[f][t]


def near_labels(rows):
    return [rows[NEAR_ROW + f : NEAR_ROW + f + 1, :] for f in range(FACES)]


def prepare_kernel(
    values,
    base,
    jac_coefs,
    proj3,
    rows,
    volume,
    face_proj,
    flux_local,
    flux_neigh,
    face_lift,
    pre_out,
    flux_out,
    near_out,
    inner3_out,
    local_coefs,
    neigh_coefs,
    lift3_out,
    near_pickers_out,
    halo_out,
    fault_pickers_out,
):
    picks = fault_pickers(rows[ELEM_ROW : ELEM_ROW + 1, :])
    fault_pickers_out[...] = jnp.concatenate(picks, axis=0)
    plan_faces(rows, near_pickers_out, halo_out)
    margin = jnp.zeros((FACE_ROWS - FACE_BASIS, BASIS), f32)
    pieces = [volume[d].T for d in range(3)]
    for f in range(FACES):
        pieces += [face_proj[3 * f], margin]
    inner3 = left3(jnp.concatenate(pieces, axis=0))
    inner3_out[...] = inner3
    build_coefs(flux_local, local_coefs)
    build_coefs(flux_neigh, neigh_coefs)
    lift3_out[...] = left3(
        jnp.concatenate(
            [piece for f in range(FACES) for piece in (face_lift[:, f, :], margin)], axis=0
        ).T
    )
    local_part(
        load_tiles(values),
        load_tiles(base),
        inner3,
        jac_coefs,
        local_coefs,
        near_pickers_out[...],
        near_labels(rows),
        proj3[...],
        (pre_out, flux_out, near_out),
    )


def again_kernel(
    values,
    base,
    jac_coefs,
    proj3,
    pickers,
    rows,
    inner3,
    local_coefs,
    pre_out,
    flux_out,
    near_out,
):
    local_part(
        load_tiles(values),
        load_tiles(base),
        inner3[...],
        jac_coefs,
        local_coefs,
        pickers[...],
        near_labels(rows),
        proj3[...],
        (pre_out, flux_out, near_out),
    )


def face_terms(twin, across, pair, beyond, halo, near, neigh_coefs, flux):
    rows = TILES * FACE_ROWS
    lane = iotas(rows, LANES)[1]
    blocks = [
        twin[...],
        across[0:rows, :],
        jnp.where(lane % WIDE < WIDE // 2, pair[0:rows, :], beyond[0:rows, :]),
    ]
    parts = [split(block) for block in blocks]
    left = jnp.concatenate(
        [
            jnp.concatenate([part[0] for part in parts], axis=1),
            jnp.concatenate([part[1] for part in parts], axis=1),
        ],
        axis=0,
    ).astype(bf16)
    moved = mm(left, halo[...])
    moved = moved[0:rows] + moved[rows : 2 * rows]
    sums = [[], [], []]
    for f in range(FACES):
        at = FACE_ROWS * f
        behind = [
            moved[FACE_ROWS * t : FACE_ROWS * (t + 1), LANES * f : LANES * (f + 1)]
            + near[t, at : at + FACE_ROWS, :]
            for t in range(TILES)
        ]
        through = contract(neigh_coefs, [(f, behind)])
        for t in range(TILES):
            sums[t].append(through[t] + flux[t, at : at + FACE_ROWS, :])
    return [jnp.concatenate(pieces, axis=0) for pieces in sums]


def lifted(pre, terms, lift3):
    lifts = mm(lift3[...], stacked(terms))
    return [pre[t] - lifts[:, LANES * t : LANES * (t + 1)] for t in range(TILES)]


def fault_pickers(fault_elem):
    sublane, lane = iotas(LANES, LANES)
    group = lane // WIDE
    source = fault_elem + jnp.where(group == 1, WIDE, 3 * WIDE)
    hit = sublane == source
    return [
        one_hot(hit & (group == 0)),
        one_hot(hit & ((group == 1) | (group == 2))),
        one_hot(hit & (group == 3)),
    ]


def middle_kernel(
    twin,
    across,
    pair,
    beyond,
    halo,
    near,
    neigh_coefs,
    flux,
    pre,
    lift3,
    first,
    second,
    stiff3,
    jac_coefs,
    pickers,
    rows,
    proj3,
    fault_picker,
    advanced_out,
    later_out,
    twin_out,
    across_out,
    depth_out,
    pair_out,
):
    terms = face_terms(twin, across, pair, beyond, halo, near, neigh_coefs, flux)
    advanced = lifted(pre, terms, lift3)
    store_tiles(advanced_out, advanced)
    repeated = integrals(advanced, stiff3[...], jac_coefs, False)[0]
    is_fast = rows[CLUSTER_ROW : CLUSTER_ROW + 1, :] == 0
    later = [jnp.where(is_fast, repeated[t], second[t]) for t in range(TILES)]
    store_tiles(later_out, later)
    parts = []
    for t in range(TILES):
        parts.append(jnp.concatenate(split(first[t] + later[t]), axis=0))
    moved = mm(jnp.concatenate(parts, axis=1).astype(bf16), fault_picker[...])
    fault = (moved[0:BASIS], moved[BASIS : 2 * BASIS]), rows[FAULT_ROW : FAULT_ROW + 1, :]
    outs = (twin_out, across_out, depth_out, pair_out)
    send(later, pickers, rows, proj3[...], outs, fault)


def final_kernel(
    twin,
    across,
    pair,
    beyond,
    halo,
    near,
    neigh_coefs,
    flux,
    pre,
    lift3,
    sent,
    rows,
    reals,
    fault_picker,
    result,
):
    at = TILES * FACE_ROWS
    own = sent[at : at + FACE_ROWS, :]
    other = pair[at : at + FACE_ROWS, :]
    limit = reals[0:1, :]
    side = reals[1:2, :]
    group = iotas(FACE_ROWS, LANES)[1] // WIDE
    mean = 0.5 * (own + other)
    jump = side * (0.5 * (other - own))
    shear = mean + pltpu.roll(jump, 2 * WIDE, 1)
    shear = jnp.where(group < 2, shear, pltpu.roll(shear, 2 * WIDE, 1))
    square = shear * shear
    mate = jnp.where(
        group % 2 == 0, pltpu.roll(square, 3 * WIDE, 1), pltpu.roll(square, WIDE, 1)
    )
    factor = limit / jnp.maximum(jnp.sqrt(square + mate), limit)
    traction = shear * factor
    jump = jnp.where(group < 2, traction, side * (traction - shear))
    face = rows[FAULT_ROW : FAULT_ROW + 1, :] // 3
    placed = jnp.concatenate([jnp.where(face == f, jump, 0.0) for f in range(FACES)], axis=0)
    spread = lax.dot_general(
        jnp.concatenate(split(placed), axis=0).astype(bf16),
        fault_picker[...],
        (((1,), (1,)), ((), ())),
        preferred_element_type=f32,
    )
    count = FACES * FACE_ROWS
    spread = spread[0:count] + spread[count : 2 * count]
    terms = face_terms(twin, across, pair, beyond, halo, near, neigh_coefs, flux)
    terms = [terms[t] - spread[:, LANES * t : LANES * (t + 1)] for t in range(TILES)]
    new = lifted(pre, terms, lift3)
    for t in range(2):
        result[LANES * t : LANES * (t + 1), :] = new[t].T
    result[2 * LANES : 2 * LANES + WIDE, :] = new[2].T[3 * WIDE : 4 * WIDE, :]


FIRST_SPARE = (24, 8, 16)
LATER_SPARE = (16, 8, 24)
COSTS = dict(place=100000, first_sends=100000, first_local=4, advance=8, later_local=4, combine=4)


def call(kernel, name, outs, *operands):
    vmem = pl.BlockSpec(memory_space=pltpu.VMEM)
    return pl.pallas_call(
        kernel,
        out_shape=[jax.ShapeDtypeStruct(shape, dtype) for shape, dtype in outs],
        in_specs=[vmem] * len(operands),
        out_specs=[vmem] * len(outs),
        compiler_params=pltpu.CompilerParams(vmem_limit_bytes=40 * 1024 * 1024),
        cost_estimate=pl.CostEstimate(
            flops=COSTS[name] * 10**6, bytes_accessed=COSTS[name] * 10**6, transcendentals=0
        ),
        name=name,
    )(*operands)


def with_twin(message, axis):
    length = lax.axis_size(axis)
    return lax.ppermute(message, axis, [(i, i ^ 1) for i in range(length)])


def with_other_side(message, axis):
    length = lax.axis_size(axis)
    pairs = [(i, (i - 1 ^ 1) + 1) for i in range(1, length - 1)]
    return lax.ppermute(message, axis, pairs)


def exchanged(twin, across, pair, beyond):
    pair = with_twin(pair, "depth")
    beyond = with_other_side(beyond, "depth")
    across = with_other_side(across, "strike")
    twin = with_twin(twin, "strike")
    return twin, across, pair, beyond


def per_device(
    state_dofs,
    jacobians,
    flux_local,
    flux_neigh,
    stiffness,
    volume,
    face_proj,
    face_lift,
    strength,
    cluster,
    neighbours,
    face_orient,
    strike_sends,
    strike_orient,
    depth_sends,
    depth_orient,
    fault_elem,
    fault_proj,
):
    quant, basis, elems = state_dofs.shape
    state = jnp.transpose(state_dofs, (0, 2, 1)).reshape(quant * elems, basis)
    jac = jnp.transpose(jacobians, (1, 2, 0, 3))
    local = jnp.transpose(flux_local, (1, 2, 0, 3))
    neigh = jnp.transpose(flux_neigh, (1, 2, 0, 3))
    proj = jnp.transpose(face_proj, (0, 2, 1))
    lift = jnp.transpose(face_lift, (1, 0, 2))
    strength, cluster, fault_elem, fault_proj = (
        array.reshape(1, -1) for array in (strength, cluster, fault_elem, fault_proj)
    )

    full = ((TILES, BASIS, LANES), f32)
    faces = ((TILES, FACES * FACE_ROWS, LANES), f32)
    coefs = ((COEFS, 4, LANES), f32)
    message = ((TILES * FACE_ROWS, LANES), f32)
    sized = [((TILES * FACE_ROWS + more, LANES), f32) for more in FIRST_SPARE]
    resized = [((TILES * FACE_ROWS + more, LANES), f32) for more in LATER_SPARE]

    (odd,) = call(place_kernel, "place", [((8, LANES), jnp.int32)])
    base, first, second, jac_coefs, stiff3, proj3, pickers, rows, reals, *messages = call(
        send_kernel,
        "first_sends",
        [
            full,
            full,
            full,
            coefs,
            ((3 * BASIS, 3 * BASIS), bf16),
            ((PROJS * FACE_ROWS, 3 * BASIS), bf16),
            ((LANES, 3 * LANES), bf16),
            ((ROWS, LANES), jnp.int32),
            ((8, LANES), f32),
            message,
            *sized,
        ],
        state,
        jac,
        stiffness,
        proj,
        odd,
        strike_sends,
        strike_orient,
        depth_sends,
        depth_orient,
        neighbours,
        face_orient,
        cluster,
        strength,
        fault_elem,
        fault_proj,
    )
    twin, across, sideways, pair = messages
    arrived = exchanged(twin, across, pair, sideways)
    pre, flux, near, inner3, local_coefs, neigh_coefs, *rest = call(
        prepare_kernel,
        "first_local",
        [
            full,
            faces,
            faces,
            ((3 * BASIS + FACES * FACE_ROWS, 3 * BASIS), bf16),
            coefs,
            coefs,
            ((BASIS, 3 * FACES * FACE_ROWS), bf16),
            ((LANES, FACES * LANES), bf16),
            ((3 * LANES, FACES * LANES), bf16),
            ((TILES * LANES, LANES), bf16),
        ],
        first,
        base,
        jac_coefs,
        proj3,
        rows,
        volume,
        proj,
        local,
        neigh,
        lift,
    )
    lift3, near_pickers, halo, fault_picker = rest
    advanced, later, twin, across, sideways, pair = call(
        middle_kernel,
        "advance",
        [full, full, message, *resized],
        *arrived,
        halo,
        near,
        neigh_coefs,
        flux,
        pre,
        lift3,
        first,
        second,
        stiff3,
        jac_coefs,
        pickers,
        rows,
        proj3,
        fault_picker,
    )
    arrived = exchanged(twin, across, pair, sideways)
    pre, flux, near = call(
        again_kernel,
        "later_local",
        [full, faces, faces],
        later,
        advanced,
        jac_coefs,
        proj3,
        near_pickers,
        rows,
        inner3,
        local_coefs,
    )
    (result,) = call(
        final_kernel,
        "combine",
        [((quant * elems, basis), f32)],
        *arrived,
        halo,
        near,
        neigh_coefs,
        flux,
        pre,
        lift3,
        pair,
        rows,
        reals,
        fault_picker,
    )
    return jnp.transpose(result.reshape(quant, elems, basis), (0, 2, 1))


def solution(mesh):
    spread = ("strike", "depth")
    placed = (
        P(None, None, spread),
        P(None, None, None, spread),
        P(None, None, None, spread),
        P(None, None, None, spread),
        P(),
        P(),
        P(),
        P(),
        P(spread),
        P(spread),
        P(None, spread),
        P(None, spread),
        P(None, spread),
        P(None, spread),
        P(None, spread),
        P(None, spread),
        P(spread),
        P(spread),
    )
    return jax.shard_map(
        per_device,
        mesh=mesh,
        in_specs=placed,
        out_specs=P(None, None, spread),
        check_vma=False,
    )
```

```python
import jax
import jax.numpy as jnp
from jax import lax
from jax.experimental import pallas as pl
from jax.experimental.pallas import tpu as pltpu
from jax.sharding import PartitionSpec as P


BASIS = 56
FACE_BASIS = 21
FACE_ROWS = 24
ORDER = 6
PROJS = 12
FACES = 4
WIDE = 32
LANES = 128
TILES = 3
COEFS = 21
FAULT_ROW, CLUSTER_ROW, ELEM_ROW, SEND_ROW, NEAR_ROW, BEHIND_ROW, ROWS = 0, 1, 2, 3, 6, 10, 16

fast_step = 0.5
f32 = jnp.float32
bf16 = jnp.bfloat16


def split(values):
    high = values.astype(bf16).astype(f32)
    return high, values - high


def right3(values):
    high, low = split(values)
    return jnp.concatenate([high, high, low], axis=0).astype(bf16)


def left3(weights):
    high, low = split(weights)
    return jnp.concatenate([high, low, high], axis=1).astype(bf16)


def mm(left, right):
    return jnp.dot(left, right, preferred_element_type=f32)


def stacked(tiles):
    return jnp.concatenate([right3(tile) for tile in tiles], axis=1)


def lane_tiled(row):
    return jnp.concatenate([row] * (LANES // row.shape[1]), axis=1)


def build_coefs(source, target):
    def across(pieces):
        return jnp.concatenate(pieces, axis=1)

    kinds = source.shape[2]
    for out in range(2):
        for into in range(2):
            for turn in range(4):
                target[(out * 2 + into) * 4 + turn, 0:kinds, :] = across(
                    [source[4 * out + (g + turn) % 4, 4 * into + g] for g in range(4)]
                )
        target[16 + out, 0:kinds, :] = across([source[4 * out + g, 8] for g in range(4)])
        target[18 + out, 0:kinds, :] = across([source[8, 4 * out + g] for g in range(4)])
    corner = source[8, 8]
    empty = jnp.zeros_like(corner)
    target[20, 0:kinds, :] = across([corner, empty, empty, empty])


def contract(coefs, terms):
    def product(slot, kind, values):
        return coefs[slot, kind : kind + 1, :] * values

    def total(products):
        result = products[0]
        for other in products[1:]:
            result = result + other
        return result

    found = []
    for out in range(2):
        sums = []
        for turn in range(4):
            products = [
                product((out * 2 + into) * 4 + turn, kind, tiles[into])
                for kind, tiles in terms
                for into in range(2)
            ]
            if turn == 0:
                products += [product(16 + out, kind, tiles[2]) for kind, tiles in terms]
            moved = total(products)
            sums.append(pltpu.roll(moved, WIDE * turn, 1) if turn else moved)
        found.append(total(sums))
    last = total(
        [product(18 + into, kind, tiles[into]) for kind, tiles in terms for into in range(2)]
        + [product(20, kind, tiles[2]) for kind, tiles in terms]
    )
    last = last + pltpu.roll(last, 2 * WIDE, 1)
    last = last + pltpu.roll(last, WIDE, 1)
    return found[0], found[1], last


def volume_like(tiles, weights3, coefs):
    whole = mm(weights3, stacked(tiles))
    applied = [whole[:, LANES * t : LANES * (t + 1)] for t in range(TILES)]
    terms = [
        (d, [part[BASIS * d : BASIS * (d + 1)] for part in applied]) for d in range(3)
    ]
    return list(contract(coefs, terms))


def integrals(tiles, weights3, coefs, with_second):
    current = tiles
    first = second = None
    factorial = 1.0
    for degree in range(ORDER):
        factorial = factorial * (degree + 1)
        early = fast_step ** (degree + 1)
        late = (2.0 * fast_step) ** (degree + 1) - early
        term = [tile * (early / factorial) for tile in current]
        first = term if first is None else [a + b for a, b in zip(first, term)]
        if with_second:
            term = [tile * (late / factorial) for tile in current]
            second = term if second is None else [a + b for a, b in zip(second, term)]
        if degree + 1 < ORDER:
            current = volume_like(current, weights3, coefs)
    return first, second


def iotas(rows, columns):
    shape = (rows, columns)
    return (
        lax.broadcasted_iota(jnp.int32, shape, 0),
        lax.broadcasted_iota(jnp.int32, shape, 1),
    )


def one_hot(mask):
    return jnp.where(mask, 1.0, 0.0).astype(bf16)


def picking(elements):
    sublane, lane = iotas(LANES, LANES)
    return one_hot(sublane == elements + (lane // WIDE) * WIDE)


def traces(gathered, labels, proj3):
    count = len(gathered)
    right = jnp.concatenate(
        [jnp.concatenate([h, h, l], axis=0).astype(bf16) for h, l in gathered], axis=1
    )
    table = mm(proj3, right)
    found = []
    for i in range(count):
        column = table[:, LANES * i : LANES * (i + 1)]
        picked = column[0:FACE_ROWS]
        for m in range(1, PROJS):
            picked = jnp.where(
                labels[i] == m, column[FACE_ROWS * m : FACE_ROWS * (m + 1)], picked
            )
        found.append(picked)
    return found


def picked_traces(tiles, pickers, labels, proj3, extra=None):
    parts = []
    for tile in tiles:
        parts.extend(split(tile))
    rows = jnp.concatenate(parts, axis=0).astype(bf16)
    moved = mm(rows, pickers)
    jobs = len(labels)
    gathered, marks = [], []
    for j in range(jobs):
        column = moved[:, LANES * j : LANES * (j + 1)]
        for t in range(TILES):
            at = 2 * BASIS * t
            gathered.append((column[at : at + BASIS], column[at + BASIS : at + 2 * BASIS]))
            marks.append(labels[j])
    if extra is not None:
        gathered.append(extra[0])
        marks.append(extra[1])
    found = traces(gathered, marks, proj3)
    picked = [found[TILES * j : TILES * (j + 1)] for j in range(jobs)]
    return picked if extra is None else (picked, found[-1])


def load_tiles(ref):
    return [ref[t] for t in range(TILES)]


def store_tiles(ref, tiles):
    for t in range(TILES):
        ref[t] = tiles[t]


def place_kernel(odd_out):
    lane = iotas(1, LANES)[1]
    for i, axis in enumerate(("strike", "depth")):
        odd_out[i : i + 1, :] = lane * 0 + lax.axis_index(axis) % 2


def either(table, odd):
    odd = odd[:, 0 : table.shape[1]]
    twin = table[1:2, :] * (1 - odd) + table[0:1, :] * odd
    across = table[0:1, :] * (1 - odd) + table[1:2, :] * odd
    return twin, across


def send_rows(strike, depth, odd):
    rows = [lane_tiled(row) for row in either(strike, odd[0:1, :])]
    rows.append(lane_tiled(jnp.concatenate(either(depth, odd[1:2, :]), axis=1)))
    return rows


def plan_faces(rows, near_pickers_out, halo_out):
    strike_odd = lax.axis_index("strike") % 2
    depth_odd = lax.axis_index("depth") % 2
    sublane, lane = iotas(LANES, LANES)
    group = (lane // WIDE) * WIDE
    for f in range(FACES):
        behind = rows[BEHIND_ROW + f : BEHIND_ROW + f + 1, :]
        columns = slice(LANES * f, LANES * (f + 1))
        local = jnp.where(behind < WIDE, behind, -4 * LANES)
        near_pickers_out[:, columns] = one_hot(sublane == local + group)
        strike_slot = (behind - WIDE) ^ (WIDE * (1 - strike_odd))
        depth_slot = (behind - 3 * WIDE) ^ ((WIDE // 2) * (1 - depth_odd))
        for block, slot in enumerate((strike_slot, strike_slot - WIDE, depth_slot)):
            if block < 2:
                inside = (behind >= WIDE) & (behind < 3 * WIDE)
            else:
                inside = (behind >= 3 * WIDE) & (behind < 4 * WIDE)
            inside = inside & (slot >= 0) & (slot < WIDE)
            slot = jnp.where(inside, slot, -4 * LANES)
            halo_out[LANES * block : LANES * (block + 1), columns] = one_hot(
                sublane == slot + group
            )


def send_kernel(
    state,
    jacobians,
    stiffness,
    face_proj,
    odd,
    strike_sends,
    strike_orient,
    depth_sends,
    depth_orient,
    neighbours,
    face_orient,
    cluster,
    strength,
    fault_elem,
    fault_proj,
    base_out,
    first_out,
    second_out,
    jac_coefs,
    stiff3_out,
    proj3_out,
    pickers_out,
    rows_out,
    reals_out,
    twin_out,
    across_out,
    depth_out,
    pair_out,
):
    build_coefs(jacobians, jac_coefs)
    stiff3 = left3(jnp.concatenate([-stiffness[d].T for d in range(3)], axis=0))
    stiff3_out[...] = stiff3
    tiles = [state[LANES * t : LANES * (t + 1), :].T for t in range(2)]
    last = state[2 * LANES : 2 * LANES + WIDE, :]
    tiles.append(jnp.concatenate([last] * 4, axis=0).T)
    store_tiles(base_out, tiles)
    first, second = integrals(tiles, stiff3, jac_coefs, True)
    store_tiles(first_out, first)
    store_tiles(second_out, second)
    margin = jnp.zeros((FACE_ROWS - FACE_BASIS, BASIS), f32)
    proj3 = left3(
        jnp.concatenate([piece for m in range(PROJS) for piece in (face_proj[m], margin)], axis=0)
    )
    proj3_out[...] = proj3
    for j, row in enumerate(send_rows(strike_sends, depth_sends, odd[...])):
        pickers_out[:, LANES * j : LANES * (j + 1)] = picking(row)
    for j, row in enumerate(send_rows(strike_orient, depth_orient, odd[...])):
        rows_out[SEND_ROW + j : SEND_ROW + j + 1, :] = row
    send(first, pickers_out, rows_out, proj3, (twin_out, across_out, depth_out, pair_out))
    rows_out[FAULT_ROW : FAULT_ROW + 1, :] = lane_tiled(fault_proj[...])
    rows_out[CLUSTER_ROW : CLUSTER_ROW + 1, :] = lane_tiled(cluster[...])
    rows_out[ELEM_ROW : ELEM_ROW + 1, :] = lane_tiled(fault_elem[...])
    for f in range(FACES):
        rows_out[NEAR_ROW + f : NEAR_ROW + f + 1, :] = lane_tiled(face_orient[f : f + 1, :])
        rows_out[BEHIND_ROW + f : BEHIND_ROW + f + 1, :] = lane_tiled(neighbours[f : f + 1, :])
    reals_out[0:1, :] = lane_tiled(strength[...])
    reals_out[1:2, :] = jnp.where(odd[1:2, :] == 0, 1.0, -1.0)


def send(values, pickers, rows, proj3, outs, extra=None):
    labels = [rows[SEND_ROW + j : SEND_ROW + j + 1, :] for j in range(3)]
    found = picked_traces(values, pickers[...], labels, proj3, extra)
    if extra is not None:
        found, own = found
    for out, pieces in zip(outs, (*found, found[2])):
        for t in range(TILES):
            out[FACE_ROWS * t : FACE_ROWS * (t + 1), :] = pieces[t]
        spare = out.shape[0] - TILES * FACE_ROWS
        if spare:
            out[TILES * FACE_ROWS :, :] = jnp.zeros((spare, LANES), f32)
    if extra is not None:
        outs[3][TILES * FACE_ROWS : TILES * FACE_ROWS + FACE_ROWS, :] = own


def local_part(values, base, vol3, jac_coefs, own3, local_coefs, pickers, labels, proj3, outs):
    pre_out, flux_out, near_out = outs
    interior = volume_like(values, vol3, jac_coefs)
    for t in range(TILES):
        pre_out[t] = base[t] + interior[t]
    own = mm(own3, stacked(values))
    for f in range(FACES):
        at = FACE_ROWS * f
        rows = own[at : at + FACE_ROWS]
        fluxes = contract(
            local_coefs, [(f, [rows[:, LANES * t : LANES * (t + 1)] for t in range(TILES)])]
        )
        for t in range(TILES):
            flux_out[t, at : at + FACE_ROWS, :] = fluxes[t]
    near = picked_traces(values, pickers, labels, proj3)
    for f in range(FACES):
        at = FACE_ROWS * f
        for t in range(TILES):
            near_out[t, at : at + FACE_ROWS, :] = near[f][t]


def near_labels(rows):
    return [rows[NEAR_ROW + f : NEAR_ROW + f + 1, :] for f in range(FACES)]


def prepare_kernel(
    values,
    base,
    jac_coefs,
    proj3,
    rows,
    volume,
    face_proj,
    flux_local,
    flux_neigh,
    face_lift,
    pre_out,
    flux_out,
    near_out,
    vol3_out,
    own3_out,
    local_coefs,
    neigh_coefs,
    lift3_out,
    near_pickers_out,
    halo_out,
    fault_pickers_out,
):
    picks = fault_pickers(rows[ELEM_ROW : ELEM_ROW + 1, :])
    fault_pickers_out[...] = jnp.concatenate(picks, axis=0)
    plan_faces(rows, near_pickers_out, halo_out)
    vol3 = left3(jnp.concatenate([volume[d].T for d in range(3)], axis=0))
    vol3_out[...] = vol3
    margin = jnp.zeros((FACE_ROWS - FACE_BASIS, BASIS), f32)
    own3 = left3(
        jnp.concatenate([piece for f in range(FACES) for piece in (face_proj[3 * f], margin)], axis=0)
    )
    own3_out[...] = own3
    build_coefs(flux_local, local_coefs)
    build_coefs(flux_neigh, neigh_coefs)
    lift3_out[...] = left3(
        jnp.concatenate(
            [piece for f in range(FACES) for piece in (face_lift[:, f, :], margin)], axis=0
        ).T
    )
    local_part(
        load_tiles(values),
        load_tiles(base),
        vol3,
        jac_coefs,
        own3,
        local_coefs,
        near_pickers_out[...],
        near_labels(rows),
        proj3[...],
        (pre_out, flux_out, near_out),
    )


def again_kernel(
    values,
    base,
    jac_coefs,
    proj3,
    pickers,
    rows,
    vol3,
    own3,
    local_coefs,
    pre_out,
    flux_out,
    near_out,
):
    local_part(
        load_tiles(values),
        load_tiles(base),
        vol3[...],
        jac_coefs,
        own3[...],
        local_coefs,
        pickers[...],
        near_labels(rows),
        proj3[...],
        (pre_out, flux_out, near_out),
    )


def face_terms(twin, across, pair, beyond, halo, near, neigh_coefs, flux):
    rows = TILES * FACE_ROWS
    lane = iotas(rows, LANES)[1]
    blocks = [
        twin[...],
        across[0:rows, :],
        jnp.where(lane % WIDE < WIDE // 2, pair[0:rows, :], beyond[0:rows, :]),
    ]
    parts = [split(block) for block in blocks]
    left = jnp.concatenate(
        [
            jnp.concatenate([part[0] for part in parts], axis=1),
            jnp.concatenate([part[1] for part in parts], axis=1),
        ],
        axis=0,
    ).astype(bf16)
    moved = mm(left, halo[...])
    moved = moved[0:rows] + moved[rows : 2 * rows]
    sums = [[], [], []]
    for f in range(FACES):
        at = FACE_ROWS * f
        behind = [
            moved[FACE_ROWS * t : FACE_ROWS * (t + 1), LANES * f : LANES * (f + 1)]
            + near[t, at : at + FACE_ROWS, :]
            for t in range(TILES)
        ]
        through = contract(neigh_coefs, [(f, behind)])
        for t in range(TILES):
            sums[t].append(through[t] + flux[t, at : at + FACE_ROWS, :])
    return [jnp.concatenate(pieces, axis=0) for pieces in sums]


def lifted(pre, terms, lift3):
    lifts = mm(lift3[...], stacked(terms))
    return [pre[t] - lifts[:, LANES * t : LANES * (t + 1)] for t in range(TILES)]


def fault_pickers(fault_elem):
    sublane, lane = iotas(LANES, LANES)
    group = lane // WIDE
    source = fault_elem + jnp.where(group == 1, WIDE, 3 * WIDE)
    hit = sublane == source
    return [
        one_hot(hit & (group == 0)),
        one_hot(hit & ((group == 1) | (group == 2))),
        one_hot(hit & (group == 3)),
    ]


def middle_kernel(
    twin,
    across,
    pair,
    beyond,
    halo,
    near,
    neigh_coefs,
    flux,
    pre,
    lift3,
    first,
    second,
    stiff3,
    jac_coefs,
    pickers,
    rows,
    proj3,
    fault_picker,
    advanced_out,
    later_out,
    twin_out,
    across_out,
    depth_out,
    pair_out,
):
    terms = face_terms(twin, across, pair, beyond, halo, near, neigh_coefs, flux)
    advanced = lifted(pre, terms, lift3)
    store_tiles(advanced_out, advanced)
    repeated = integrals(advanced, stiff3[...], jac_coefs, False)[0]
    is_fast = rows[CLUSTER_ROW : CLUSTER_ROW + 1, :] == 0
    later = [jnp.where(is_fast, repeated[t], second[t]) for t in range(TILES)]
    store_tiles(later_out, later)
    parts = []
    for t in range(TILES):
        parts.append(jnp.concatenate(split(first[t] + later[t]), axis=0))
    moved = mm(jnp.concatenate(parts, axis=1).astype(bf16), fault_picker[...])
    fault = (moved[0:BASIS], moved[BASIS : 2 * BASIS]), rows[FAULT_ROW : FAULT_ROW + 1, :]
    outs = (twin_out, across_out, depth_out, pair_out)
    send(later, pickers, rows, proj3[...], outs, fault)


def final_kernel(
    twin,
    across,
    pair,
    beyond,
    halo,
    near,
    neigh_coefs,
    flux,
    pre,
    lift3,
    sent,
    rows,
    reals,
    fault_picker,
    result,
):
    at = TILES * FACE_ROWS
    own = sent[at : at + FACE_ROWS, :]
    other = pair[at : at + FACE_ROWS, :]
    limit = reals[0:1, :]
    side = reals[1:2, :]
    group = iotas(FACE_ROWS, LANES)[1] // WIDE
    mean = 0.5 * (own + other)
    jump = side * (0.5 * (other - own))
    shear = mean + pltpu.roll(jump, 2 * WIDE, 1)
    shear = jnp.where(group < 2, shear, pltpu.roll(shear, 2 * WIDE, 1))
    square = shear * shear
    mate = jnp.where(
        group % 2 == 0, pltpu.roll(square, 3 * WIDE, 1), pltpu.roll(square, WIDE, 1)
    )
    factor = limit / jnp.maximum(jnp.sqrt(square + mate), limit)
    traction = shear * factor
    jump = jnp.where(group < 2, traction, side * (traction - shear))
    face = rows[FAULT_ROW : FAULT_ROW + 1, :] // 3
    placed = jnp.concatenate([jnp.where(face == f, jump, 0.0) for f in range(FACES)], axis=0)
    spread = lax.dot_general(
        jnp.concatenate(split(placed), axis=0).astype(bf16),
        fault_picker[...],
        (((1,), (1,)), ((), ())),
        preferred_element_type=f32,
    )
    count = FACES * FACE_ROWS
    spread = spread[0:count] + spread[count : 2 * count]
    terms = face_terms(twin, across, pair, beyond, halo, near, neigh_coefs, flux)
    terms = [terms[t] - spread[:, LANES * t : LANES * (t + 1)] for t in range(TILES)]
    new = lifted(pre, terms, lift3)
    for t in range(2):
        result[LANES * t : LANES * (t + 1), :] = new[t].T
    result[2 * LANES : 2 * LANES + WIDE, :] = new[2].T[3 * WIDE : 4 * WIDE, :]


FIRST_SPARE = (24, 8, 16)
LATER_SPARE = (16, 8, 24)
COSTS = dict(place=100000, first_sends=100000, first_local=4, advance=8, later_local=4, combine=4)


def call(kernel, name, outs, *operands):
    vmem = pl.BlockSpec(memory_space=pltpu.VMEM)
    return pl.pallas_call(
        kernel,
        out_shape=[jax.ShapeDtypeStruct(shape, dtype) for shape, dtype in outs],
        in_specs=[vmem] * len(operands),
        out_specs=[vmem] * len(outs),
        compiler_params=pltpu.CompilerParams(vmem_limit_bytes=40 * 1024 * 1024),
        cost_estimate=pl.CostEstimate(
            flops=COSTS[name] * 10**6, bytes_accessed=COSTS[name] * 10**6, transcendentals=0
        ),
        name=name,
    )(*operands)


def with_twin(message, axis):
    length = lax.axis_size(axis)
    return lax.ppermute(message, axis, [(i, i ^ 1) for i in range(length)])


def with_other_side(message, axis):
    length = lax.axis_size(axis)
    pairs = [(i, (i - 1 ^ 1) + 1) for i in range(1, length - 1)]
    return lax.ppermute(message, axis, pairs)


def exchanged(twin, across, pair, beyond):
    pair = with_twin(pair, "depth")
    beyond = with_other_side(beyond, "depth")
    across = with_other_side(across, "strike")
    twin = with_twin(twin, "strike")
    return twin, across, pair, beyond


def per_device(
    state_dofs,
    jacobians,
    flux_local,
    flux_neigh,
    stiffness,
    volume,
    face_proj,
    face_lift,
    strength,
    cluster,
    neighbours,
    face_orient,
    strike_sends,
    strike_orient,
    depth_sends,
    depth_orient,
    fault_elem,
    fault_proj,
):
    quant, basis, elems = state_dofs.shape
    state = jnp.transpose(state_dofs, (0, 2, 1)).reshape(quant * elems, basis)
    jac = jnp.transpose(jacobians, (1, 2, 0, 3))
    local = jnp.transpose(flux_local, (1, 2, 0, 3))
    neigh = jnp.transpose(flux_neigh, (1, 2, 0, 3))
    proj = jnp.transpose(face_proj, (0, 2, 1))
    lift = jnp.transpose(face_lift, (1, 0, 2))
    strength, cluster, fault_elem, fault_proj = (
        array.reshape(1, -1) for array in (strength, cluster, fault_elem, fault_proj)
    )

    full = ((TILES, BASIS, LANES), f32)
    faces = ((TILES, FACES * FACE_ROWS, LANES), f32)
    coefs = ((COEFS, 4, LANES), f32)
    message = ((TILES * FACE_ROWS, LANES), f32)
    sized = [((TILES * FACE_ROWS + more, LANES), f32) for more in FIRST_SPARE]
    resized = [((TILES * FACE_ROWS + more, LANES), f32) for more in LATER_SPARE]

    (odd,) = call(place_kernel, "place", [((8, LANES), jnp.int32)])
    base, first, second, jac_coefs, stiff3, proj3, pickers, rows, reals, *messages = call(
        send_kernel,
        "first_sends",
        [
            full,
            full,
            full,
            coefs,
            ((3 * BASIS, 3 * BASIS), bf16),
            ((PROJS * FACE_ROWS, 3 * BASIS), bf16),
            ((LANES, 3 * LANES), bf16),
            ((ROWS, LANES), jnp.int32),
            ((8, LANES), f32),
            message,
            *sized,
        ],
        state,
        jac,
        stiffness,
        proj,
        odd,
        strike_sends,
        strike_orient,
        depth_sends,
        depth_orient,
        neighbours,
        face_orient,
        cluster,
        strength,
        fault_elem,
        fault_proj,
    )
    twin, across, sideways, pair = messages
    arrived = exchanged(twin, across, pair, sideways)
    pre, flux, near, vol3, own3, local_coefs, neigh_coefs, *rest = call(
        prepare_kernel,
        "first_local",
        [
            full,
            faces,
            faces,
            ((3 * BASIS, 3 * BASIS), bf16),
            ((FACES * FACE_ROWS, 3 * BASIS), bf16),
            coefs,
            coefs,
            ((BASIS, 3 * FACES * FACE_ROWS), bf16),
            ((LANES, FACES * LANES), bf16),
            ((3 * LANES, FACES * LANES), bf16),
            ((TILES * LANES, LANES), bf16),
        ],
        first,
        base,
        jac_coefs,
        proj3,
        rows,
        volume,
        proj,
        local,
        neigh,
        lift,
    )
    lift3, near_pickers, halo, fault_picker = rest
    advanced, later, twin, across, sideways, pair = call(
        middle_kernel,
        "advance",
        [full, full, message, *resized],
        *arrived,
        halo,
        near,
        neigh_coefs,
        flux,
        pre,
        lift3,
        first,
        second,
        stiff3,
        jac_coefs,
        pickers,
        rows,
        proj3,
        fault_picker,
    )
    arrived = exchanged(twin, across, pair, sideways)
    pre, flux, near = call(
        again_kernel,
        "later_local",
        [full, faces, faces],
        later,
        advanced,
        jac_coefs,
        proj3,
        near_pickers,
        rows,
        vol3,
        own3,
        local_coefs,
    )
    (result,) = call(
        final_kernel,
        "combine",
        [((quant * elems, basis), f32)],
        *arrived,
        halo,
        near,
        neigh_coefs,
        flux,
        pre,
        lift3,
        pair,
        rows,
        reals,
        fault_picker,
    )
    return jnp.transpose(result.reshape(quant, elems, basis), (0, 2, 1))


def solution(mesh):
    spread = ("strike", "depth")
    placed = (
        P(None, None, spread),
        P(None, None, None, spread),
        P(None, None, None, spread),
        P(None, None, None, spread),
        P(),
        P(),
        P(),
        P(),
        P(spread),
        P(spread),
        P(None, spread),
        P(None, spread),
        P(None, spread),
        P(None, spread),
        P(None, spread),
        P(None, spread),
        P(spread),
        P(spread),
    )
    return jax.shard_map(
        per_device,
        mesh=mesh,
        in_specs=placed,
        out_specs=P(None, None, spread),
        check_vma=False,
    )
```
